512 devices in a mesh: section: 16 (over z, core), dp: 32 (over x, y).
Axes of the slice: x: 4, y: 8, z: 8, core: 2. Of those that a mesh axis runs over, the one named last changes fastest.
Arguments:
- grads: bfloat16 [16, 32, 80, 8192], P('section', 'dp'), may hold values from -6400 to 6400
- owners: int32 [16, 24], P('section'), may hold values from 0 to 31, as said below
- master: float32 [16, 32, 8, 8192], P('section', 'dp'), may hold values from -0.008 to 0.008
- moment: float32 [16, 32, 8, 8192], P('section', 'dp'), may hold values from -4 to 4
- second: float32 [16, 32, 8, 8192], P('section', 'dp'), may hold values from 0.01 to 1
- average: float32 [16, 32, 8, 8192], P('section', 'dp'), may hold values from -0.0001 to 0.0001
Outputs:
- weights: bfloat16 [16, 80, 8192], P('section')
- master_out: float32 [16, 32, 8, 8192], P('section', 'dp')
- moment_out: float32 [16, 32, 8, 8192], P('section', 'dp')
- second_out: float32 [16, 32, 8, 8192], P('section', 'dp')
- average_out: float32 [16, 32, 8, 8192], P('section', 'dp')
The draws below stay inside these ranges and needn't reach their ends.
Inputs may be any that keep to these rules, and one draw needn't show every extreme that they name: The 24 tensors of one section have 24 different owners.
All inputs are finite; a program needn't handle non-finite values.
Results may differ from the reference program's by a relative error of at most 0.012.
Values may be sent and summed in bfloat16 or wider, within the bound.
No kernel may reach another device: no remote copies, remote signals or barrier semaphores. Data moves between devices by JAX's collectives and lax.ppermute only.
A program may use at most 64 MiB of HBM per device.

```python
import math
import jax
import jax.numpy as jnp
from jax import lax

D = 8192
LAYERS = 4
ALLROWS = 80
CAP = 8
TENSORS = 24
STEP = 10
SECTIONS = 16
N_DP = 32


def draw_grads(key, part):
    key = jax.random.fold_in(key, 11)
    first, rowkey, colkey = jax.random.split(key, 3)
    shape = (SECTIONS, N_DP, ALLROWS, D)
    section_scale = (1.0 + 2.0 * jnp.arange(SECTIONS, dtype=jnp.float32) / max(SECTIONS - 1, 1)).reshape(SECTIONS, 1, 1, 1)
    row_scale = jnp.exp(jax.random.uniform(rowkey, (SECTIONS, 1, ALLROWS, 1), jnp.float32) * math.log(10.0))
    rising = 1.0 + 2.0 * jnp.arange(D, dtype=jnp.float32) / (D - 1)
    col_scale = (jnp.exp(jax.random.uniform(colkey, (D,), jnp.float32) * math.log(10.0)) * rising).reshape(1, 1, 1, D)
    base = jax.random.truncated_normal(first, -4.0, 4.0, shape, jnp.float32)
    return (base * section_scale * row_scale * col_scale).astype(jnp.bfloat16)


def draw_owners(key, part):
    key = jax.random.fold_in(key, 7)
    section_keys = jax.random.split(key, SECTIONS)

    def pick(section_key):
        return jax.random.permutation(section_key, N_DP)[:TENSORS]
    picked = jax.vmap(pick)(section_keys)
    first_key, order_key = jax.random.split(jax.random.fold_in(key, 1))
    others = 1 + jax.random.permutation(first_key, N_DP - 2)[:TENSORS - 2]
    ends = jnp.array([N_DP - 1, 0], dtype=jnp.int32)
    leading = jax.random.permutation(order_key, jnp.concatenate([ends, others.astype(jnp.int32)]))
    picked = picked.astype(jnp.int32).at[0].set(leading)
    return picked.astype(jnp.int32)


def draw_master(key, part):
    key = jax.random.fold_in(key, 21)
    shape = (SECTIONS, N_DP, CAP, D)
    base = jax.random.truncated_normal(key, -4.0, 4.0, shape, jnp.float32)
    return (0.002 * base).astype(jnp.float32)


def draw_average(key, part):
    key = jax.random.fold_in(key, 23)
    shape = (SECTIONS, N_DP, CAP, D)
    base = jax.random.truncated_normal(key, -4.0, 4.0, shape, jnp.float32)
    return (2e-05 * base).astype(jnp.float32)


def level_of(stream_key, dims, cuts, low, top_value):
    level, own = 1.0, jax.random.fold_in(stream_key, 6)
    for dim, parts in cuts:
        steps = jnp.exp(jax.random.uniform(jax.random.fold_in(own, dim), (parts,), jnp.float32, low / len(cuts), top_value / len(cuts)))
        level = level * jnp.repeat(steps, dims[dim] // parts).reshape([-1 if axis == dim else 1 for axis in range(len(dims))])
    return level


def gaussian(rng, extent, width, most, cuts=(), kind=jnp.bfloat16):
    factor_of = level_of(rng, extent, cuts, -0.22, 0.18) if cuts else 1.0
    drawn = jax.random.normal(rng, extent, jnp.float32) * width * factor_of
    return jnp.minimum(jnp.maximum(drawn, -most), most).astype(kind)


def setup_inputs(seed: int = 0) -> dict:
    key_of = jax.random.split(jax.random.key(seed), 7)
    grads = draw_grads(jax.random.fold_in(key_of[6], 71), 0)
    owners = draw_owners(jax.random.fold_in(key_of[6], 71), 0)
    master = draw_master(jax.random.fold_in(key_of[6], 71), 0)
    moment = gaussian(key_of[3], (SECTIONS, N_DP, CAP, D), 0.3, 4.0, ((0, 16), (1, 32)), jnp.float32)
    second = jnp.clip(jnp.exp(math.log(1.0) - 4.6051702 * jax.random.uniform(key_of[4], (SECTIONS, N_DP, CAP, D), jnp.float32) ** level_of(key_of[4], (SECTIONS, N_DP, CAP, D), ((0, 16), (1, 32)), -0.2, 0.2)), 0.01, 1.0)
    average = draw_average(jax.random.fold_in(key_of[6], 71), 0)
    return dict(grads=grads, owners=owners, master=master, moment=moment, second=second, average=average)


beta_one = 0.9
beta_two = 0.95
epsilon = 1e-08
learn_rate = 0.0003
decay_rate = 0.1
average_keep = 0.999
clip_level = 0.5

def tensor_layout(all_rows, slot_rows, layers):
    layer_rows = all_rows // layers
    kv_rows = (layer_rows - 2 - 2 * slot_rows) // 2
    counts = [slot_rows, kv_rows, kv_rows, slot_rows, 1, 1]
    layout = []
    start = 0
    for layer in range(layers):
        for position, count in enumerate(counts):
            layout.append((start, count, 1.0 if position < 4 else 0.0))
            start = start + count
    return layout

def adamw(grad, master, moment, second, average, decay, factor):
    clipped = factor * grad
    moment_new = beta_one * moment + (1.0 - beta_one) * clipped
    second_new = beta_two * second + (1.0 - beta_two) * clipped * clipped
    direction = moment_new / (1.0 - beta_one ** STEP) / (jnp.sqrt(second_new / (1.0 - beta_two ** STEP)) + epsilon)
    master_new = master - learn_rate * (direction + decay_rate * decay * master)
    average_new = average_keep * average + (1.0 - average_keep) * master_new
    return (master_new, moment_new, second_new, average_new)

def reference(grads, owners, master, moment, second, average):
    layout = tensor_layout(ALLROWS, CAP, LAYERS)
    means = lax.optimization_barrier(jnp.sum(grads.astype(jnp.float32), axis=1)) / N_DP
    squares = jnp.sum(means * means)
    factor = jnp.minimum(1.0, clip_level / jnp.sqrt(squares / (SECTIONS * ALLROWS * D) + 1e-06))

    def one_section(mean, owner, master_s, moment_s, second_s, average_s):
        zero = jnp.zeros((), jnp.int32)
        bucket = jnp.zeros((N_DP, CAP, D), jnp.float32)
        used = jnp.zeros((N_DP, CAP, 1), jnp.float32)
        decay = jnp.zeros((N_DP, CAP, 1), jnp.float32)
        for tensor, (start, count, flag) in enumerate(layout):
            rows = jnp.pad(mean[start:start + count], ((0, CAP - count), (0, 0)))
            marks = (jnp.arange(CAP) < count).astype(jnp.float32).reshape(1, CAP, 1)
            where_at = (owner[tensor].astype(jnp.int32), zero, zero)
            bucket = lax.dynamic_update_slice(bucket, rows[None], where_at)
            used = lax.dynamic_update_slice(used, marks, where_at)
            decay = lax.dynamic_update_slice(decay, marks * flag, where_at)
        fresh = adamw(bucket, master_s, moment_s, second_s, average_s, decay, factor)
        olds = (master_s, moment_s, second_s, average_s)
        kept = tuple((jnp.where(used > 0.5, new_value, old_value) for new_value, old_value in zip(fresh, olds)))
        pieces = []
        for tensor, (start, count, flag) in enumerate(layout):
            block = lax.dynamic_index_in_dim(kept[0], owner[tensor].astype(jnp.int32), 0, keepdims=False)
            pieces.append(block[:count])
        weights = jnp.concatenate(pieces, axis=0).astype(jnp.bfloat16)
        return (weights, kept[0], kept[1], kept[2], kept[3])
    result = jax.vmap(one_section)(means, owners, master, moment, second, average)
    return (result[0], result[1], result[2], result[3], result[4])
```

```python
import functools

import jax
import jax.numpy as jnp
from jax import lax
from jax.experimental import pallas as pl
from jax.experimental.pallas import tpu as pltpu
from jax.sharding import PartitionSpec as P

STEP = 10

beta_one = 0.9
beta_two = 0.95
epsilon = 1e-08
learn_rate = 0.0003
decay_rate = 0.1
average_keep = 0.999
clip_level = 0.5

XS = 4
YS = 8
CORES = 2


def tensor_layout(all_rows, slot_rows, layers):
    layer_rows = all_rows // layers
    kv_rows = (layer_rows - 2 - 2 * slot_rows) // 2
    counts = [slot_rows, kv_rows, kv_rows, slot_rows, 1, 1]
    layout = []
    start = 0
    for layer in range(layers):
        for position, count in enumerate(counts):
            layout.append((start, count, 1.0 if position < 4 else 0.0))
            start = start + count
    return layout


def adamw_moments(grad, moment, second, factor):
    clipped = factor * grad
    moment_new = beta_one * moment + (1.0 - beta_one) * clipped
    second_new = beta_two * second + (1.0 - beta_two) * clipped * clipped
    return moment_new, second_new


def adamw_master(master, moment_new, second_new, decay):
    direction = (
        moment_new
        / (1.0 - beta_one**STEP)
        / (jnp.sqrt(second_new / (1.0 - beta_two**STEP)) + epsilon)
    )
    return master - learn_rate * (direction + decay_rate * decay * master)


def clip_factor(squares, numel):
    return jnp.minimum(1.0, clip_level / jnp.sqrt(squares / numel + 1e-06))


def split_kernel(layout, replicas, owner, parts, master, moment, second, mean, payload):
    rows, width = mean.shape
    total = parts[0].astype(jnp.float32)
    for part in range(1, parts.shape[0]):
        total = total + parts[part].astype(jnp.float32)
    own = total / replicas
    mean[...] = own
    squared = own * own
    partial = squared[0:8]
    for row in range(8, rows, 8):
        partial = partial + squared[row : row + 8]
    partial = partial[:, :128] + partial[:, 128:]
    high = partial.astype(jnp.bfloat16)
    low = (partial - high.astype(jnp.float32)).astype(jnp.bfloat16)
    squares = jnp.concatenate(
        [high.astype(jnp.float32), low.astype(jnp.float32)], axis=1
    )
    zeros = jnp.zeros((8, width), jnp.float32)
    empty = jnp.concatenate([zeros, squares], axis=0).astype(jnp.bfloat16)
    for device in range(replicas):
        columns = slice(device * width, (device + 1) * width)
        payload[device, 0:16, :] = empty
        payload[device, 16:32, :] = jnp.concatenate(
            [moment[:, columns], second[:, columns]], axis=0
        ).astype(jnp.bfloat16)
        whole = master[:, columns]
        top = whole.astype(jnp.bfloat16).astype(jnp.float32)
        payload[device, 32:48, :] = jnp.concatenate(
            [top, whole - top], axis=0
        ).astype(jnp.bfloat16)
    for tensor, (start, count, flag) in enumerate(layout):
        block = mean[start : start + count, :]
        if count < 8:
            block = jnp.concatenate(
                [block, jnp.zeros((8 - count, width), jnp.float32)], axis=0
            )
        payload[owner[tensor], 0:16, :] = jnp.concatenate(
            [block, squares], axis=0
        ).astype(jnp.bfloat16)


def column_kernel(layout, numel, owner, squares, mean, received, copies, master, moment, second, decay):
    factor = clip_factor(jnp.sum(squares[...]), numel)
    for tensor, (start, count, flag) in enumerate(layout):
        root = owner[tensor]
        slots = received[root, 16:32, :].astype(jnp.float32)
        halves = received[root, 32:48, :].astype(jnp.float32)
        rows = slice(start, start + count)
        moment[rows, :] = slots[:count]
        second[rows, :] = slots[8 : 8 + count]
        master[rows, :] = halves[:count] + halves[8 : 8 + count]
        decay[rows, :] = jnp.full((count, decay.shape[1]), flag, jnp.float32)
    moment_new, second_new = adamw_moments(mean[...], moment[...], second[...], factor)
    weights = adamw_master(master[...], moment_new, second_new, decay[...])
    weights = weights.astype(jnp.bfloat16)
    for copy in range(copies.shape[0]):
        copies[copy] = weights


def owner_kernel(
    layout, numel, owner, me, squares, received, master, moment, second, average,
    master_out, moment_out, second_out, average_out,
):
    factor = clip_factor(jnp.sum(squares[...]), numel)
    count = jnp.int32(0)
    flag = jnp.float32(0.0)
    for tensor, (start, rows, decay) in enumerate(layout):
        mine = owner[tensor] == me[0]
        count = jnp.where(mine, rows, count)
        flag = jnp.where(mine, decay, flag)
    width = received.shape[2]
    used = lax.broadcasted_iota(jnp.int32, (8, width), 0) < count
    for source in range(received.shape[0]):
        columns = slice(source * width, (source + 1) * width)
        grad = received[source, 0:16, :].astype(jnp.float32)[0:8]
        olds = (master[:, columns], moment[:, columns], second[:, columns], average[:, columns])
        moment_new, second_new = adamw_moments(grad, olds[1], olds[2], factor)
        master_new = adamw_master(olds[0], moment_new, second_new, flag)
        average_new = average_keep * olds[3] + (1.0 - average_keep) * master_new
        master_out[:, columns] = jnp.where(used, master_new, olds[0])
        moment_out[:, columns] = jnp.where(used, moment_new, olds[1])
        second_out[:, columns] = jnp.where(used, second_new, olds[2])
        average_out[:, columns] = jnp.where(used, average_new, olds[3])


VMEM = pl.BlockSpec(memory_space=pltpu.VMEM)
SMEM = pl.BlockSpec(memory_space=pltpu.SMEM)
LIMIT = 32 * 1024 * 1024


def local(grads, owners, master, moment, second, average):
    rows = grads.shape[2]
    width = grads.shape[3]
    layout = tensor_layout(rows, master.shape[2], owners.shape[1] // 6)
    replicas = lax.axis_size("dp")
    sections = lax.axis_size("section")
    numel = sections * rows * width
    owner = owners[0]
    own_index = lax.axis_index("dp").astype(jnp.int32).reshape(1)
    along_x = [[x * YS + y for x in range(XS)] for y in range(YS)]
    along_y = [[x * YS + y for y in range(YS)] for x in range(XS)]
    along_z = [list(range(core, sections, CORES)) for core in range(CORES)]
    pairs = [[z * CORES + core for core in range(CORES)] for z in range(sections // CORES)]
    exchange = functools.partial(lax.all_to_all, split_axis=0, concat_axis=0, tiled=True)
    params = pltpu.CompilerParams(vmem_limit_bytes=LIMIT)
    olds = (master[0, 0], moment[0, 0], second[0, 0], average[0, 0])
    narrow = width // replicas
    wide = width // XS

    with jax.named_scope("reduce_x"):
        blocks = grads[0, 0].reshape(rows, XS, wide).transpose(1, 0, 2)
        blocks = exchange(blocks, "dp", axis_index_groups=along_x)
        summed = jnp.sum(blocks.astype(jnp.float32), axis=0).astype(jnp.bfloat16)
    with jax.named_scope("reduce_y"):
        blocks = summed.reshape(rows, YS, narrow).transpose(1, 0, 2)
        blocks = exchange(blocks, "dp", axis_index_groups=along_y)
    with jax.named_scope("split"):
        mean, payload = pl.pallas_call(
            functools.partial(split_kernel, layout, replicas),
            out_shape=(
                jax.ShapeDtypeStruct((rows, narrow), jnp.float32),
                jax.ShapeDtypeStruct((replicas, 48, narrow), jnp.bfloat16),
            ),
            in_specs=[SMEM, VMEM, VMEM, VMEM, VMEM],
            out_specs=(VMEM, VMEM),
            compiler_params=params,
        )(owner, blocks, olds[0], olds[1], olds[2])
    with jax.named_scope("to_owners"):
        received = exchange(payload, "dp")
    with jax.named_scope("squares"):
        squares = jnp.sum(received[:, 8:16, :].astype(jnp.float32), axis=0)
        squares = squares[:, :128] + squares[:, 128:]
        squares = jnp.broadcast_to(squares, (sections // CORES,) + squares.shape)
        squares = exchange(squares, "section", axis_index_groups=along_z)
        squares = lax.all_gather(squares, "section", axis_index_groups=pairs, tiled=True)
    with jax.named_scope("columns"):
        copies = pl.pallas_call(
            functools.partial(column_kernel, layout, numel),
            out_shape=jax.ShapeDtypeStruct((YS, rows, narrow), jnp.bfloat16),
            in_specs=[SMEM, VMEM, VMEM, VMEM],
            out_specs=VMEM,
            scratch_shapes=[pltpu.VMEM((rows, narrow), jnp.float32)] * 4,
            compiler_params=params,
        )(owner, squares, mean, received)
    with jax.named_scope("gather_y"):
        gathered = exchange(copies, "dp", axis_index_groups=along_y)
    with jax.named_scope("gather_x"):
        copies = jnp.broadcast_to(gathered, (XS,) + gathered.shape)
        gathered = exchange(copies, "dp", axis_index_groups=along_x)
        weights = gathered.transpose(2, 0, 1, 3).reshape(rows, width)
    with jax.named_scope("owned"):
        state = jax.ShapeDtypeStruct(olds[0].shape, jnp.float32)
        news = pl.pallas_call(
            functools.partial(owner_kernel, layout, numel),
            out_shape=(state,) * 4,
            in_specs=[SMEM, SMEM] + [VMEM] * 6,
            out_specs=(VMEM,) * 4,
            compiler_params=params,
        )(owner, own_index, squares, received, *olds)
    return (weights[None],) + tuple(new[None, None] for new in news)


def solution(mesh):
    in_specs = (
        P("section", "dp", None, None),
        P("section", None),
        P("section", "dp", None, None),
        P("section", "dp", None, None),
        P("section", "dp", None, None),
        P("section", "dp", None, None),
    )
    out_specs = (
        P("section", None, None),
        P("section", "dp", None, None),
        P("section", "dp", None, None),
        P("section", "dp", None, None),
        P("section", "dp", None, None),
    )
    return jax.shard_map(local, mesh=mesh, in_specs=in_specs, out_specs=out_specs, check_vma=False)
```

```python
import functools

import jax
import jax.numpy as jnp
from jax import lax
from jax.experimental import pallas as pl
from jax.experimental.pallas import tpu as pltpu
from jax.sharding import PartitionSpec as P

STEP = 10

beta_one = 0.9
beta_two = 0.95
epsilon = 1e-08
learn_rate = 0.0003
decay_rate = 0.1
average_keep = 0.999
clip_level = 0.5

XS = 4
YS = 8
CORES = 2


def tensor_layout(all_rows, slot_rows, layers):
    layer_rows = all_rows // layers
    kv_rows = (layer_rows - 2 - 2 * slot_rows) // 2
    counts = [slot_rows, kv_rows, kv_rows, slot_rows, 1, 1]
    layout = []
    start = 0
    for layer in range(layers):
        for position, count in enumerate(counts):
            layout.append((start, count, 1.0 if position < 4 else 0.0))
            start = start + count
    return layout


def adamw_moments(grad, moment, second, factor):
    clipped = factor * grad
    moment_new = beta_one * moment + (1.0 - beta_one) * clipped
    second_new = beta_two * second + (1.0 - beta_two) * clipped * clipped
    return moment_new, second_new


def adamw_master(master, moment_new, second_new, decay):
    direction = (
        moment_new
        / (1.0 - beta_one**STEP)
        / (jnp.sqrt(second_new / (1.0 - beta_two**STEP)) + epsilon)
    )
    return master - learn_rate * (direction + decay_rate * decay * master)


def clip_factor(squares, numel):
    return jnp.minimum(1.0, clip_level / jnp.sqrt(squares / numel + 1e-06))


def split_kernel(layout, replicas, owner, parts, master, moment, second, mean, payload):
    rows, width = mean.shape
    total = parts[0].astype(jnp.float32)
    for part in range(1, parts.shape[0]):
        total = total + parts[part].astype(jnp.float32)
    own = total / replicas
    mean[...] = own
    squared = own * own
    partial = squared[0:8]
    for row in range(8, rows, 8):
        partial = partial + squared[row : row + 8]
    partial = partial[:, :128] + partial[:, 128:]
    high = partial.astype(jnp.bfloat16)
    low = (partial - high.astype(jnp.float32)).astype(jnp.bfloat16)
    squares = jnp.concatenate(
        [high.astype(jnp.float32), low.astype(jnp.float32)], axis=1
    )
    zeros = jnp.zeros((8, width), jnp.float32)
    empty = jnp.concatenate([zeros, squares], axis=0).astype(jnp.bfloat16)
    for device in range(replicas):
        columns = slice(device * width, (device + 1) * width)
        payload[device, 0:16, :] = empty
        payload[device, 16:32, :] = jnp.concatenate(
            [moment[:, columns], second[:, columns]], axis=0
        ).astype(jnp.bfloat16)
        whole = master[:, columns]
        top = whole.astype(jnp.bfloat16).astype(jnp.float32)
        payload[device, 32:48, :] = jnp.concatenate(
            [top, whole - top], axis=0
        ).astype(jnp.bfloat16)
    for tensor, (start, count, flag) in enumerate(layout):
        block = mean[start : start + count, :]
        if count < 8:
            block = jnp.concatenate(
                [block, jnp.zeros((8 - count, width), jnp.float32)], axis=0
            )
        payload[owner[tensor], 0:16, :] = jnp.concatenate(
            [block, squares], axis=0
        ).astype(jnp.bfloat16)


def column_kernel(layout, numel, owner, squares, mean, received, copies, master, moment, second, decay):
    factor = clip_factor(jnp.sum(squares[...]), numel)
    for tensor, (start, count, flag) in enumerate(layout):
        root = owner[tensor]
        slots = received[root, 16:32, :].astype(jnp.float32)
        halves = received[root, 32:48, :].astype(jnp.float32)
        rows = slice(start, start + count)
        moment[rows, :] = slots[:count]
        second[rows, :] = slots[8 : 8 + count]
        master[rows, :] = halves[:count] + halves[8 : 8 + count]
        decay[rows, :] = jnp.full((count, decay.shape[1]), flag, jnp.float32)
    moment_new, second_new = adamw_moments(mean[...], moment[...], second[...], factor)
    weights = adamw_master(master[...], moment_new, second_new, decay[...])
    weights = weights.astype(jnp.bfloat16)
    for copy in range(copies.shape[0]):
        copies[copy] = weights


def owner_kernel(
    layout, numel, owner, me, squares, received, master, moment, second, average,
    master_out, moment_out, second_out, average_out,
):
    factor = clip_factor(jnp.sum(squares[...]), numel)
    count = jnp.int32(0)
    flag = jnp.float32(0.0)
    for tensor, (start, rows, decay) in enumerate(layout):
        mine = owner[tensor] == me[0]
        count = jnp.where(mine, rows, count)
        flag = jnp.where(mine, decay, flag)
    width = received.shape[2]
    used = lax.broadcasted_iota(jnp.int32, (8, width), 0) < count
    for source in range(received.shape[0]):
        columns = slice(source * width, (source + 1) * width)
        grad = received[source, 0:16, :].astype(jnp.float32)[0:8]
        olds = (master[:, columns], moment[:, columns], second[:, columns], average[:, columns])
        moment_new, second_new = adamw_moments(grad, olds[1], olds[2], factor)
        master_new = adamw_master(olds[0], moment_new, second_new, flag)
        average_new = average_keep * olds[3] + (1.0 - average_keep) * master_new
        master_out[:, columns] = jnp.where(used, master_new, olds[0])
        moment_out[:, columns] = jnp.where(used, moment_new, olds[1])
        second_out[:, columns] = jnp.where(used, second_new, olds[2])
        average_out[:, columns] = jnp.where(used, average_new, olds[3])


def cut_kernel(grads, blocks, sems):
    parts, _, width = blocks.shape
    moves = [
        pltpu.make_async_copy(
            grads.at[0, 0, :, pl.ds(part * width, width)], blocks.at[part], sems.at[part]
        )
        for part in range(parts)
    ]
    for move in moves:
        move.start()
    for move in moves:
        move.wait()


def copies_kernel(block, copies):
    for copy in range(copies.shape[0]):
        copies[copy] = block[...]


def join_kernel(blocks, weights, sems):
    parts, _, width = blocks.shape
    moves = [
        pltpu.make_async_copy(
            blocks.at[part], weights.at[0, :, pl.ds(part * width, width)], sems.at[part]
        )
        for part in range(parts)
    ]
    for move in moves:
        move.start()
    for move in moves:
        move.wait()


VMEM = pl.BlockSpec(memory_space=pltpu.VMEM)
HBM = pl.BlockSpec(memory_space=pltpu.HBM)
SMEM = pl.BlockSpec(memory_space=pltpu.SMEM)
LIMIT = 32 * 1024 * 1024


def local(grads, owners, master, moment, second, average):
    rows = grads.shape[2]
    width = grads.shape[3]
    layout = tensor_layout(rows, master.shape[2], owners.shape[1] // 6)
    replicas = lax.axis_size("dp")
    sections = lax.axis_size("section")
    numel = sections * rows * width
    owner = owners[0]
    own_index = lax.axis_index("dp").astype(jnp.int32).reshape(1)
    along_x = [[x * YS + y for x in range(XS)] for y in range(YS)]
    along_y = [[x * YS + y for y in range(YS)] for x in range(XS)]
    along_z = [list(range(core, sections, CORES)) for core in range(CORES)]
    pairs = [[z * CORES + core for core in range(CORES)] for z in range(sections // CORES)]
    exchange = functools.partial(lax.all_to_all, split_axis=0, concat_axis=0, tiled=True)
    params = pltpu.CompilerParams(vmem_limit_bytes=LIMIT)
    olds = (master[0, 0], moment[0, 0], second[0, 0], average[0, 0])
    narrow = width // replicas
    wide = width // XS

    with jax.named_scope("reduce_x"):
        blocks = pl.pallas_call(
            cut_kernel,
            out_shape=jax.ShapeDtypeStruct((XS, rows, wide), jnp.bfloat16),
            in_specs=[HBM],
            out_specs=VMEM,
            scratch_shapes=[pltpu.SemaphoreType.DMA((XS,))],
            compiler_params=pltpu.CompilerParams(vmem_limit_bytes=LIMIT),
        )(grads)
        blocks = exchange(blocks, "dp", axis_index_groups=along_x)
        summed = jnp.sum(blocks.astype(jnp.float32), axis=0).astype(jnp.bfloat16)
    with jax.named_scope("reduce_y"):
        blocks = summed.reshape(rows, YS, narrow).transpose(1, 0, 2)
        blocks = exchange(blocks, "dp", axis_index_groups=along_y)
    with jax.named_scope("split"):
        mean, payload = pl.pallas_call(
            functools.partial(split_kernel, layout, replicas),
            out_shape=(
                jax.ShapeDtypeStruct((rows, narrow), jnp.float32),
                jax.ShapeDtypeStruct((replicas, 48, narrow), jnp.bfloat16),
            ),
            in_specs=[SMEM, VMEM, VMEM, VMEM, VMEM],
            out_specs=(VMEM, VMEM),
            compiler_params=params,
        )(owner, blocks, olds[0], olds[1], olds[2])
    with jax.named_scope("to_owners"):
        received = exchange(payload, "dp")
    with jax.named_scope("squares"):
        squares = jnp.sum(received[:, 8:16, :].astype(jnp.float32), axis=0)
        squares = squares[:, :128] + squares[:, 128:]
        squares = jnp.broadcast_to(squares, (sections // CORES,) + squares.shape)
        squares = exchange(squares, "section", axis_index_groups=along_z)
        squares = lax.all_gather(squares, "section", axis_index_groups=pairs, tiled=True)
    with jax.named_scope("columns"):
        copies = pl.pallas_call(
            functools.partial(column_kernel, layout, numel),
            out_shape=jax.ShapeDtypeStruct((YS, rows, narrow), jnp.bfloat16),
            in_specs=[SMEM, VMEM, VMEM, VMEM],
            out_specs=VMEM,
            scratch_shapes=[pltpu.VMEM((rows, narrow), jnp.float32)] * 4,
            compiler_params=params,
        )(owner, squares, mean, received)
    with jax.named_scope("gather_y"):
        gathered = exchange(copies, "dp", axis_index_groups=along_y)
    with jax.named_scope("gather_x"):
        copies = pl.pallas_call(
            copies_kernel,
            out_shape=jax.ShapeDtypeStruct((XS,) + gathered.shape, jnp.bfloat16),
            in_specs=[VMEM],
            out_specs=VMEM,
            compiler_params=params,
        )(gathered)
        gathered = exchange(copies, "dp", axis_index_groups=along_x)
    with jax.named_scope("join"):
        weights = pl.pallas_call(
            join_kernel,
            out_shape=jax.ShapeDtypeStruct((1, rows, width), jnp.bfloat16),
            in_specs=[VMEM],
            out_specs=HBM,
            scratch_shapes=[pltpu.SemaphoreType.DMA((replicas,))],
            compiler_params=params,
        )(gathered.reshape(replicas, rows, narrow))
    with jax.named_scope("owned"):
        state = jax.ShapeDtypeStruct(olds[0].shape, jnp.float32)
        news = pl.pallas_call(
            functools.partial(owner_kernel, layout, numel),
            out_shape=(state,) * 4,
            in_specs=[SMEM, SMEM] + [VMEM] * 6,
            out_specs=(VMEM,) * 4,
            compiler_params=params,
        )(owner, own_index, squares, received, *olds)
    return (weights,) + tuple(new[None, None] for new in news)


def solution(mesh):
    in_specs = (
        P("section", "dp", None, None),
        P("section", None),
        P("section", "dp", None, None),
        P("section", "dp", None, None),
        P("section", "dp", None, None),
        P("section", "dp", None, None),
    )
    out_specs = (
        P("section", None, None),
        P("section", "dp", None, None),
        P("section", "dp", None, None),
        P("section", "dp", None, None),
        P("section", "dp", None, None),
    )
    return jax.shard_map(local, mesh=mesh, in_specs=in_specs, out_specs=out_specs, check_vma=False)
```

```python
import functools

import jax
import jax.numpy as jnp
from jax import lax
from jax.experimental import pallas as pl
from jax.experimental.pallas import tpu as pltpu
from jax.sharding import PartitionSpec as P

STEP = 10

beta_one = 0.9
beta_two = 0.95
epsilon = 1e-08
learn_rate = 0.0003
decay_rate = 0.1
average_keep = 0.999
clip_level = 0.5

XS = 4
YS = 8
CORES = 2


def tensor_layout(all_rows, slot_rows, layers):
    layer_rows = all_rows // layers
    kv_rows = (layer_rows - 2 - 2 * slot_rows) // 2
    counts = [slot_rows, kv_rows, kv_rows, slot_rows, 1, 1]
    layout = []
    start = 0
    for layer in range(layers):
        for position, count in enumerate(counts):
            layout.append((start, count, 1.0 if position < 4 else 0.0))
            start = start + count
    return layout


def adamw_moments(grad, moment, second, factor):
    clipped = factor * grad
    moment_new = beta_one * moment + (1.0 - beta_one) * clipped
    second_new = beta_two * second + (1.0 - beta_two) * clipped * clipped
    return moment_new, second_new


def adamw_master(master, moment_new, second_new, decay):
    direction = (
        moment_new
        / (1.0 - beta_one**STEP)
        / (jnp.sqrt(second_new / (1.0 - beta_two**STEP)) + epsilon)
    )
    return master - learn_rate * (direction + decay_rate * decay * master)


def clip_factor(squares, numel):
    return jnp.minimum(1.0, clip_level / jnp.sqrt(squares / numel + 1e-06))


def split_kernel(layout, replicas, owner, parts, master, moment, second, mean, payload):
    rows, width = mean.shape
    half = width // 2
    total = parts[0].astype(jnp.float32)
    for part in range(1, parts.shape[0]):
        total = total + parts[part].astype(jnp.float32)
    own = total / replicas
    mean[...] = own
    squared = own * own
    partial = squared[0:8]
    for row in range(8, rows, 8):
        partial = partial + squared[row : row + 8]
    partial = partial[:, :half] + partial[:, half:]
    partial = partial[0:4] + partial[4:8]
    high = partial.astype(jnp.bfloat16).astype(jnp.float32)
    squares = jnp.concatenate([high, partial - high], axis=0).astype(jnp.bfloat16)
    empty = jnp.zeros((16, half), jnp.bfloat16)
    for device in range(replicas):
        payload[device, 0:16, :] = empty
        for place, state in enumerate((moment, second, master)):
            block = jnp.concatenate(
                [
                    state[:, device * width : device * width + half],
                    state[:, device * width + half : (device + 1) * width],
                ],
                axis=0,
            )
            payload[device, 16 * place + 16 : 16 * place + 32, :] = block.astype(jnp.bfloat16)
        payload[device, 64:72, :] = squares
    for tensor, (start, count, flag) in enumerate(layout):
        block = mean[start : start + count, :]
        if count < 8:
            block = jnp.concatenate(
                [block, jnp.zeros((8 - count, width), jnp.float32)], axis=0
            )
        payload[owner[tensor], 0:16, :] = jnp.concatenate(
            [block[:, :half], block[:, half:]], axis=0
        ).astype(jnp.bfloat16)


def column_kernel(layout, numel, owner, squares, mean, received, copies, master, moment, second, decay):
    factor = clip_factor(jnp.sum(squares[...]), numel)
    half = mean.shape[1] // 2
    for tensor, (start, count, flag) in enumerate(layout):
        root = owner[tensor]
        rows = slice(start, start + count)
        for place, state in enumerate((moment, second, master)):
            block = received[root, 16 * place + 16 : 16 * place + 32, :].astype(jnp.float32)
            state[rows, :half] = block[:count]
            state[rows, half:] = block[8 : 8 + count]
        decay[rows, :] = jnp.full((count, decay.shape[1]), flag, jnp.float32)
    moment_new, second_new = adamw_moments(mean[...], moment[...], second[...], factor)
    weights = adamw_master(master[...], moment_new, second_new, decay[...])
    weights = weights.astype(jnp.bfloat16)
    for copy in range(copies.shape[0]):
        copies[copy] = weights


def owner_kernel(
    layout, numel, owner, me, squares, received, master, moment, second, average,
    master_out, moment_out, second_out, average_out,
):
    factor = clip_factor(jnp.sum(squares[...]), numel)
    count = jnp.int32(0)
    flag = jnp.float32(0.0)
    for tensor, (start, rows, decay) in enumerate(layout):
        mine = owner[tensor] == me[0]
        count = jnp.where(mine, rows, count)
        flag = jnp.where(mine, decay, flag)
    width = 2 * received.shape[2]
    used = lax.broadcasted_iota(jnp.int32, (8, width), 0) < count
    for source in range(received.shape[0]):
        columns = slice(source * width, (source + 1) * width)
        grad = received[source, 0:16, :].astype(jnp.float32)
        grad = jnp.concatenate([grad[0:8], grad[8:16]], axis=1)
        olds = (master[:, columns], moment[:, columns], second[:, columns], average[:, columns])
        moment_new, second_new = adamw_moments(grad, olds[1], olds[2], factor)
        master_new = adamw_master(olds[0], moment_new, second_new, flag)
        average_new = average_keep * olds[3] + (1.0 - average_keep) * master_new
        master_out[:, columns] = jnp.where(used, master_new, olds[0])
        moment_out[:, columns] = jnp.where(used, moment_new, olds[1])
        second_out[:, columns] = jnp.where(used, second_new, olds[2])
        average_out[:, columns] = jnp.where(used, average_new, olds[3])


def cut_kernel(grads, blocks, sems):
    parts, _, width = blocks.shape
    moves = [
        pltpu.make_async_copy(
            grads.at[0, 0, :, pl.ds(part * width, width)], blocks.at[part], sems.at[part]
        )
        for part in range(parts)
    ]
    for move in moves:
        move.start()
    for move in moves:
        move.wait()


def join_kernel(me, *refs):
    blocks, (weights, sems) = refs[:-2], refs[-2:]
    count, _, width = blocks[0].shape
    own = lax.div(me[0], count)
    moves = []
    for step, block in enumerate(blocks):
        source = lax.rem(own + (len(blocks) - step), len(blocks))
        for part in range(count):
            start = pl.multiple_of((source * count + part) * width, width)
            moves.append(
                pltpu.make_async_copy(
                    block.at[part], weights.at[0, :, pl.ds(start, width)], sems.at[step, part]
                )
            )
    for move in moves:
        move.start()
    for move in moves:
        move.wait()


VMEM = pl.BlockSpec(memory_space=pltpu.VMEM)
HBM = pl.BlockSpec(memory_space=pltpu.HBM)
SMEM = pl.BlockSpec(memory_space=pltpu.SMEM)
LIMIT = 32 * 1024 * 1024


def local(grads, owners, master, moment, second, average):
    rows = grads.shape[2]
    width = grads.shape[3]
    layout = tensor_layout(rows, master.shape[2], owners.shape[1] // 6)
    replicas = lax.axis_size("dp")
    sections = lax.axis_size("section")
    numel = sections * rows * width
    owner = owners[0]
    own_index = lax.axis_index("dp").astype(jnp.int32).reshape(1)
    along_x = [[x * YS + y for x in range(XS)] for y in range(YS)]
    along_y = [[x * YS + y for y in range(YS)] for x in range(XS)]
    along_z = [list(range(core, sections, CORES)) for core in range(CORES)]
    pairs = [[z * CORES + core for core in range(CORES)] for z in range(sections // CORES)]
    exchange = functools.partial(lax.all_to_all, split_axis=0, concat_axis=0, tiled=True)
    params = pltpu.CompilerParams(vmem_limit_bytes=LIMIT)
    olds = (master[0, 0], moment[0, 0], second[0, 0], average[0, 0])
    narrow = width // replicas
    wide = width // XS

    with jax.named_scope("reduce_x"):
        blocks = pl.pallas_call(
            cut_kernel,
            out_shape=jax.ShapeDtypeStruct((XS, rows, wide), jnp.bfloat16),
            in_specs=[HBM],
            out_specs=VMEM,
            scratch_shapes=[pltpu.SemaphoreType.DMA((XS,))],
            compiler_params=pltpu.CompilerParams(vmem_limit_bytes=LIMIT),
        )(grads)
        blocks = exchange(blocks, "dp", axis_index_groups=along_x)
        summed = jnp.sum(blocks.astype(jnp.float32), axis=0).astype(jnp.bfloat16)
    with jax.named_scope("reduce_y"):
        blocks = summed.reshape(rows, YS, narrow).transpose(1, 0, 2)
        blocks = exchange(blocks, "dp", axis_index_groups=along_y)
    with jax.named_scope("split"):
        mean, payload = pl.pallas_call(
            functools.partial(split_kernel, layout, replicas),
            out_shape=(
                jax.ShapeDtypeStruct((rows, narrow), jnp.float32),
                jax.ShapeDtypeStruct((replicas, 72, narrow // 2), jnp.bfloat16),
            ),
            in_specs=[SMEM, VMEM, VMEM, VMEM, VMEM],
            out_specs=(VMEM, VMEM),
            compiler_params=params,
        )(owner, blocks, olds[0], olds[1], olds[2])
    with jax.named_scope("to_owners"):
        received = exchange(payload, "dp")
    with jax.named_scope("squares"):
        squares = jnp.sum(received[:, 64:72, :].astype(jnp.float32), axis=0)
        squares = jnp.broadcast_to(squares, (sections // CORES,) + squares.shape)
        squares = exchange(squares, "section", axis_index_groups=along_z)
        squares = lax.all_gather(squares, "section", axis_index_groups=pairs, tiled=True)
    with jax.named_scope("columns"):
        copies = pl.pallas_call(
            functools.partial(column_kernel, layout, numel),
            out_shape=jax.ShapeDtypeStruct((YS, rows, narrow), jnp.bfloat16),
            in_specs=[SMEM, VMEM, VMEM, VMEM],
            out_specs=VMEM,
            scratch_shapes=[pltpu.VMEM((rows, narrow), jnp.float32)] * 4,
            compiler_params=params,
        )(owner, squares, mean, received)
    with jax.named_scope("gather_y"):
        gathered = exchange(copies, "dp", axis_index_groups=along_y)
    with jax.named_scope("gather_x"):
        pieces = [gathered]
        for step in range(1, XS):
            pairs_x = [
                (x * YS + y, (x + step) % XS * YS + y) for x in range(XS) for y in range(YS)
            ]
            pieces.append(lax.ppermute(gathered, "dp", pairs_x))
    with jax.named_scope("join"):
        weights = pl.pallas_call(
            join_kernel,
            out_shape=jax.ShapeDtypeStruct((1, rows, width), jnp.bfloat16),
            in_specs=[SMEM] + [VMEM] * XS,
            out_specs=HBM,
            scratch_shapes=[pltpu.SemaphoreType.DMA((XS, YS))],
            compiler_params=params,
        )(own_index, *pieces)
    with jax.named_scope("owned"):
        state = jax.ShapeDtypeStruct(olds[0].shape, jnp.float32)
        news = pl.pallas_call(
            functools.partial(owner_kernel, layout, numel),
            out_shape=(state,) * 4,
            in_specs=[SMEM, SMEM] + [VMEM] * 6,
            out_specs=(VMEM,) * 4,
            compiler_params=params,
        )(owner, own_index, squares, received, *olds)
    return (weights,) + tuple(new[None, None] for new in news)


def solution(mesh):
    in_specs = (
        P("section", "dp", None, None),
        P("section", None),
        P("section", "dp", None, None),
        P("section", "dp", None, None),
        P("section", "dp", None, None),
        P("section", "dp", None, None),
    )
    out_specs = (
        P("section", None, None),
        P("section", "dp", None, None),
        P("section", "dp", None, None),
        P("section", "dp", None, None),
        P("section", "dp", None, None),
    )
    return jax.shard_map(local, mesh=mesh, in_specs=in_specs, out_specs=out_specs, check_vma=False)
```

```python
import functools

import jax
import jax.numpy as jnp
from jax import lax
from jax.experimental import pallas as pl
from jax.experimental.pallas import tpu as pltpu
from jax.sharding import PartitionSpec as P

STEP = 10

beta_one = 0.9
beta_two = 0.95
epsilon = 1e-08
learn_rate = 0.0003
decay_rate = 0.1
average_keep = 0.999
clip_level = 0.5

def tensor_layout(all_rows, slot_rows, layers):
    layer_rows = all_rows // layers
    kv_rows = (layer_rows - 2 - 2 * slot_rows) // 2
    counts = [slot_rows, kv_rows, kv_rows, slot_rows, 1, 1]
    layout = []
    start = 0
    for layer in range(layers):
        for position, count in enumerate(counts):
            layout.append((start, count, 1.0 if position < 4 else 0.0))
            start = start + count
    return layout


def adamw_moments(grad, moment, second, factor):
    clipped = factor * grad
    moment_new = beta_one * moment + (1.0 - beta_one) * clipped
    second_new = beta_two * second + (1.0 - beta_two) * clipped * clipped
    return moment_new, second_new


def adamw_master(master, moment_new, second_new, decay):
    direction = (
        moment_new
        / (1.0 - beta_one**STEP)
        / (jnp.sqrt(second_new / (1.0 - beta_two**STEP)) + epsilon)
    )
    return master - learn_rate * (direction + decay_rate * decay * master)


def clip_factor(squares, numel):
    return jnp.minimum(1.0, clip_level / jnp.sqrt(squares / numel + 1e-06))


def split_kernel(layout, replicas, owner, parts, master, moment, second, mean, payload):
    rows, width = mean.shape
    half = width // 2
    total = parts[0].astype(jnp.float32)
    for part in range(1, parts.shape[0]):
        total = total + parts[part].astype(jnp.float32)
    own = total / replicas
    mean[...] = own
    squared = own * own
    partial = squared[0:8]
    for row in range(8, rows, 8):
        partial = partial + squared[row : row + 8]
    partial = partial[:, :half] + partial[:, half:]
    partial = partial[0:4] + partial[4:8]
    high = partial.astype(jnp.bfloat16).astype(jnp.float32)
    squares = jnp.concatenate([high, partial - high], axis=0).astype(jnp.bfloat16)
    empty = jnp.zeros((16, half), jnp.bfloat16)
    for device in range(replicas):
        payload[device, 0:16, :] = empty
        for place, state in enumerate((moment, second, master)):
            block = jnp.concatenate(
                [
                    state[:, device * width : device * width + half],
                    state[:, device * width + half : (device + 1) * width],
                ],
                axis=0,
            )
            payload[device, 16 * place + 16 : 16 * place + 32, :] = block.astype(jnp.bfloat16)
        payload[device, 64:72, :] = squares
    for tensor, (start, count, flag) in enumerate(layout):
        block = mean[start : start + count, :]
        if count < 8:
            block = jnp.concatenate(
                [block, jnp.zeros((8 - count, width), jnp.float32)], axis=0
            )
        payload[owner[tensor], 0:16, :] = jnp.concatenate(
            [block[:, :half], block[:, half:]], axis=0
        ).astype(jnp.bfloat16)


def column_kernel(layout, numel, owner, squares, mean, received, copies, master, moment, second, decay):
    factor = clip_factor(jnp.sum(squares[...]), numel)
    half = mean.shape[1] // 2
    for tensor, (start, count, flag) in enumerate(layout):
        root = owner[tensor]
        rows = slice(start, start + count)
        for place, state in enumerate((moment, second, master)):
            block = received[root, 16 * place + 16 : 16 * place + 32, :].astype(jnp.float32)
            state[rows, :half] = block[:count]
            state[rows, half:] = block[8 : 8 + count]
        decay[rows, :] = jnp.full((count, decay.shape[1]), flag, jnp.float32)
    moment_new, second_new = adamw_moments(mean[...], moment[...], second[...], factor)
    weights = adamw_master(master[...], moment_new, second_new, decay[...])
    weights = weights.astype(jnp.bfloat16)
    for copy in range(copies.shape[0]):
        copies[copy] = weights


def owner_kernel(
    layout, numel, owner, me, squares, received, master, moment, second, average,
    master_out, moment_out, second_out, average_out,
):
    factor = clip_factor(jnp.sum(squares[...]), numel)
    count = jnp.int32(0)
    flag = jnp.float32(0.0)
    for tensor, (start, rows, decay) in enumerate(layout):
        mine = owner[tensor] == me[0]
        count = jnp.where(mine, rows, count)
        flag = jnp.where(mine, decay, flag)
    width = 2 * received.shape[2]
    used = lax.broadcasted_iota(jnp.int32, (8, width), 0) < count
    for source in range(received.shape[0]):
        columns = slice(source * width, (source + 1) * width)
        grad = received[source, 0:16, :].astype(jnp.float32)
        grad = jnp.concatenate([grad[0:8], grad[8:16]], axis=1)
        olds = (master[:, columns], moment[:, columns], second[:, columns], average[:, columns])
        moment_new, second_new = adamw_moments(grad, olds[1], olds[2], factor)
        master_new = adamw_master(olds[0], moment_new, second_new, flag)
        average_new = average_keep * olds[3] + (1.0 - average_keep) * master_new
        master_out[:, columns] = jnp.where(used, master_new, olds[0])
        moment_out[:, columns] = jnp.where(used, moment_new, olds[1])
        second_out[:, columns] = jnp.where(used, second_new, olds[2])
        average_out[:, columns] = jnp.where(used, average_new, olds[3])


def cut_kernel(grads, blocks, sems):
    parts, _, width = blocks.shape
    moves = [
        pltpu.make_async_copy(
            grads.at[0, 0, :, pl.ds(part * width, width)], blocks.at[part], sems.at[part]
        )
        for part in range(parts)
    ]
    for move in moves:
        move.start()
    for move in moves:
        move.wait()


def join_kernel(blocks, weights, sems):
    parts, _, width = blocks.shape
    moves = [
        pltpu.make_async_copy(
            blocks.at[part], weights.at[0, :, pl.ds(part * width, width)], sems.at[part]
        )
        for part in range(parts)
    ]
    for move in moves:
        move.start()
    for move in moves:
        move.wait()


VMEM = pl.BlockSpec(memory_space=pltpu.VMEM)
HBM = pl.BlockSpec(memory_space=pltpu.HBM)
SMEM = pl.BlockSpec(memory_space=pltpu.SMEM)
LIMIT = 32 * 1024 * 1024


def local(grads, owners, master, moment, second, average):
    rows = grads.shape[2]
    width = grads.shape[3]
    layout = tensor_layout(rows, master.shape[2], owners.shape[1] // 6)
    replicas = lax.axis_size("dp")
    sections = lax.axis_size("section")
    numel = sections * rows * width
    owner = owners[0]
    own_index = lax.axis_index("dp").astype(jnp.int32).reshape(1)
    exchange = functools.partial(lax.all_to_all, split_axis=0, concat_axis=0, tiled=True)
    params = pltpu.CompilerParams(vmem_limit_bytes=LIMIT)
    olds = (master[0, 0], moment[0, 0], second[0, 0], average[0, 0])
    narrow = width // replicas

    with jax.named_scope("reduce"):
        blocks = pl.pallas_call(
            cut_kernel,
            out_shape=jax.ShapeDtypeStruct((replicas, rows, narrow), jnp.bfloat16),
            in_specs=[HBM],
            out_specs=VMEM,
            scratch_shapes=[pltpu.SemaphoreType.DMA((replicas,))],
            compiler_params=params,
        )(grads)
        blocks = exchange(blocks, "dp")
    with jax.named_scope("split"):
        mean, payload = pl.pallas_call(
            functools.partial(split_kernel, layout, replicas),
            out_shape=(
                jax.ShapeDtypeStruct((rows, narrow), jnp.float32),
                jax.ShapeDtypeStruct((replicas, 72, narrow // 2), jnp.bfloat16),
            ),
            in_specs=[SMEM, VMEM, VMEM, VMEM, VMEM],
            out_specs=(VMEM, VMEM),
            compiler_params=params,
        )(owner, blocks, olds[0], olds[1], olds[2])
    with jax.named_scope("to_owners"):
        received = exchange(payload, "dp")
    with jax.named_scope("squares"):
        squares = jnp.sum(received[:, 64:72, :].astype(jnp.float32), axis=0)
        squares = jnp.broadcast_to(squares, (sections,) + squares.shape)
        squares = exchange(squares, "section")
    with jax.named_scope("columns"):
        copies = pl.pallas_call(
            functools.partial(column_kernel, layout, numel),
            out_shape=jax.ShapeDtypeStruct((replicas, rows, narrow), jnp.bfloat16),
            in_specs=[SMEM, VMEM, VMEM, VMEM],
            out_specs=VMEM,
            scratch_shapes=[pltpu.VMEM((rows, narrow), jnp.float32)] * 4,
            compiler_params=params,
        )(owner, squares, mean, received)
    with jax.named_scope("gather"):
        gathered = exchange(copies, "dp")
        weights = pl.pallas_call(
            join_kernel,
            out_shape=jax.ShapeDtypeStruct((1, rows, width), jnp.bfloat16),
            in_specs=[VMEM],
            out_specs=HBM,
            scratch_shapes=[pltpu.SemaphoreType.DMA((replicas,))],
            compiler_params=params,
        )(gathered)
    with jax.named_scope("owned"):
        state = jax.ShapeDtypeStruct(olds[0].shape, jnp.float32)
        news = pl.pallas_call(
            functools.partial(owner_kernel, layout, numel),
            out_shape=(state,) * 4,
            in_specs=[SMEM, SMEM] + [VMEM] * 6,
            out_specs=(VMEM,) * 4,
            compiler_params=params,
        )(owner, own_index, squares, received, *olds)
    return (weights,) + tuple(new[None, None] for new in news)


def solution(mesh):
    in_specs = (
        P("section", "dp", None, None),
        P("section", None),
        P("section", "dp", None, None),
        P("section", "dp", None, None),
        P("section", "dp", None, None),
        P("section", "dp", None, None),
    )
    out_specs = (
        P("section", None, None),
        P("section", "dp", None, None),
        P("section", "dp", None, None),
        P("section", "dp", None, None),
        P("section", "dp", None, None),
    )
    return jax.shard_map(local, mesh=mesh, in_specs=in_specs, out_specs=out_specs, check_vma=False)
```

```python
import functools

import jax
import jax.numpy as jnp
from jax import lax
from jax.experimental import pallas as pl
from jax.experimental.pallas import tpu as pltpu
from jax.sharding import PartitionSpec as P

STEP = 10

beta_one = 0.9
beta_two = 0.95
epsilon = 1e-08
learn_rate = 0.0003
decay_rate = 0.1
average_keep = 0.999
clip_level = 0.5

XS = 4
YS = 8


def tensor_layout(all_rows, slot_rows, layers):
    layer_rows = all_rows // layers
    kv_rows = (layer_rows - 2 - 2 * slot_rows) // 2
    counts = [slot_rows, kv_rows, kv_rows, slot_rows, 1, 1]
    layout = []
    start = 0
    for layer in range(layers):
        for position, count in enumerate(counts):
            layout.append((start, count, 1.0 if position < 4 else 0.0))
            start = start + count
    return layout


def adamw_moments(grad, moment, second, factor):
    clipped = factor * grad
    moment_new = beta_one * moment + (1.0 - beta_one) * clipped
    second_new = beta_two * second + (1.0 - beta_two) * clipped * clipped
    return moment_new, second_new


def adamw_master(master, moment_new, second_new, decay):
    direction = (
        moment_new
        / (1.0 - beta_one**STEP)
        / (jnp.sqrt(second_new / (1.0 - beta_two**STEP)) + epsilon)
    )
    return master - learn_rate * (direction + decay_rate * decay * master)


def clip_factor(squares, numel):
    return jnp.minimum(1.0, clip_level / jnp.sqrt(squares / numel + 1e-06))


def split_kernel(layout, replicas, owner, parts, master, moment, second, mean, payload):
    rows, width = mean.shape
    half = width // 2
    total = parts[0].astype(jnp.float32)
    for part in range(1, parts.shape[0]):
        total = total + parts[part].astype(jnp.float32)
    own = total / replicas
    mean[...] = own
    squared = own * own
    partial = squared[0:8]
    for row in range(8, rows, 8):
        partial = partial + squared[row : row + 8]
    partial = partial[:, :half] + partial[:, half:]
    partial = partial[0:4] + partial[4:8]
    high = partial.astype(jnp.bfloat16).astype(jnp.float32)
    squares = jnp.concatenate([high, partial - high], axis=0).astype(jnp.bfloat16)
    empty = jnp.zeros((16, half), jnp.bfloat16)
    for device in range(replicas):
        payload[device, 0:16, :] = empty
        for place, state in enumerate((moment, second, master)):
            block = jnp.concatenate(
                [
                    state[:, device * width : device * width + half],
                    state[:, device * width + half : (device + 1) * width],
                ],
                axis=0,
            )
            payload[device, 16 * place + 16 : 16 * place + 32, :] = block.astype(jnp.bfloat16)
        payload[device, 64:72, :] = squares
    for tensor, (start, count, flag) in enumerate(layout):
        block = mean[start : start + count, :]
        if count < 8:
            block = jnp.concatenate(
                [block, jnp.zeros((8 - count, width), jnp.float32)], axis=0
            )
        payload[owner[tensor], 0:16, :] = jnp.concatenate(
            [block[:, :half], block[:, half:]], axis=0
        ).astype(jnp.bfloat16)


def column_kernel(layout, numel, owner, squares, mean, received, copies, master, moment, second, decay):
    factor = clip_factor(jnp.sum(squares[...]), numel)
    half = mean.shape[1] // 2
    for tensor, (start, count, flag) in enumerate(layout):
        root = owner[tensor]
        rows = slice(start, start + count)
        for place, state in enumerate((moment, second, master)):
            block = received[root, 16 * place + 16 : 16 * place + 32, :].astype(jnp.float32)
            state[rows, :half] = block[:count]
            state[rows, half:] = block[8 : 8 + count]
        decay[rows, :] = jnp.full((count, decay.shape[1]), flag, jnp.float32)
    moment_new, second_new = adamw_moments(mean[...], moment[...], second[...], factor)
    weights = adamw_master(master[...], moment_new, second_new, decay[...])
    weights = weights.astype(jnp.bfloat16)
    for copy in range(copies.shape[0]):
        copies[copy] = weights


def finish_kernel(
    layout, numel, owner, squares, received, master, moment, second, average, blocks,
    weights, master_out, moment_out, second_out, average_out,
    master_new, moment_new, second_new, average_new, weight_sems, state_sems,
):
    parts, _, width = blocks.shape
    moves = []
    for part in range(parts):
        moves.append(
            pltpu.make_async_copy(
                blocks.at[part], weights.at[0, :, pl.ds(part * width, width)], weight_sems.at[part]
            )
        )
        moves[-1].start()
    factor = clip_factor(jnp.sum(squares[...]), numel)
    me = lax.axis_index("dp")
    count = jnp.int32(0)
    flag = jnp.float32(0.0)
    for tensor, (start, rows, decay) in enumerate(layout):
        mine = owner[tensor] == me
        count = jnp.where(mine, rows, count)
        flag = jnp.where(mine, decay, flag)
    used = lax.broadcasted_iota(jnp.int32, (8, width), 0) < count
    pairs = (
        (master_new, master_out), (moment_new, moment_out),
        (second_new, second_out), (average_new, average_out),
    )
    pieces = 4
    stretch = parts * width // pieces
    for piece in range(pieces):
        for source in range(piece * parts // pieces, (piece + 1) * parts // pieces):
            columns = slice(source * width, (source + 1) * width)
            grad = received[source, 0:16, :].astype(jnp.float32)
            grad = jnp.concatenate([grad[0:8], grad[8:16]], axis=1)
            olds = (
                master[0, 0, :, columns], moment[0, 0, :, columns],
                second[0, 0, :, columns], average[0, 0, :, columns],
            )
            first, squared = adamw_moments(grad, olds[1], olds[2], factor)
            whole = adamw_master(olds[0], first, squared, flag)
            mixed = average_keep * olds[3] + (1.0 - average_keep) * whole
            for (target, _), new, old in zip(pairs, (whole, first, squared, mixed), olds):
                target[:, columns] = jnp.where(used, new, old)
        for place, (source, target) in enumerate(pairs):
            columns = pl.ds(piece * stretch, stretch)
            moves.append(
                pltpu.make_async_copy(
                    source.at[:, columns], target.at[0, 0, :, columns], state_sems.at[place, piece]
                )
            )
            moves[-1].start()
    for move in moves:
        move.wait()


def cut_kernel(grads, blocks, sems):
    parts, _, width = blocks.shape
    moves = [
        pltpu.make_async_copy(
            grads.at[0, 0, :, pl.ds(part * width, width)], blocks.at[part], sems.at[part]
        )
        for part in range(parts)
    ]
    for move in moves:
        move.start()
    for move in moves:
        move.wait()


def copies_kernel(block, copies):
    for copy in range(copies.shape[0]):
        copies[copy] = block[...]


VMEM = pl.BlockSpec(memory_space=pltpu.VMEM)
HBM = pl.BlockSpec(memory_space=pltpu.HBM)
SMEM = pl.BlockSpec(memory_space=pltpu.SMEM)
LIMIT = 32 * 1024 * 1024


def local(grads, owners, master, moment, second, average):
    rows = grads.shape[2]
    width = grads.shape[3]
    layout = tensor_layout(rows, master.shape[2], owners.shape[1] // 6)
    replicas = lax.axis_size("dp")
    sections = lax.axis_size("section")
    numel = sections * rows * width
    owner = owners[0]
    along_x = [[x * YS + y for x in range(XS)] for y in range(YS)]
    along_y = [[x * YS + y for y in range(YS)] for x in range(XS)]
    exchange = functools.partial(lax.all_to_all, split_axis=0, concat_axis=0, tiled=True)
    params = pltpu.CompilerParams(vmem_limit_bytes=LIMIT)
    olds = (master[0, 0], moment[0, 0], second[0, 0], average[0, 0])
    narrow = width // replicas
    wide = width // XS

    with jax.named_scope("reduce_x"):
        blocks = pl.pallas_call(
            cut_kernel,
            out_shape=jax.ShapeDtypeStruct((XS, rows, wide), jnp.bfloat16),
            in_specs=[HBM],
            out_specs=VMEM,
            scratch_shapes=[pltpu.SemaphoreType.DMA((XS,))],
            compiler_params=pltpu.CompilerParams(vmem_limit_bytes=LIMIT),
        )(grads)
        blocks = exchange(blocks, "dp", axis_index_groups=along_x)
        summed = jnp.sum(blocks.astype(jnp.float32), axis=0).astype(jnp.bfloat16)
    with jax.named_scope("reduce_y"):
        blocks = summed.reshape(rows, YS, narrow).transpose(1, 0, 2)
        blocks = exchange(blocks, "dp", axis_index_groups=along_y)
    with jax.named_scope("split"):
        mean, payload = pl.pallas_call(
            functools.partial(split_kernel, layout, replicas),
            out_shape=(
                jax.ShapeDtypeStruct((rows, narrow), jnp.float32),
                jax.ShapeDtypeStruct((replicas, 72, narrow // 2), jnp.bfloat16),
            ),
            in_specs=[SMEM, VMEM, VMEM, VMEM, VMEM],
            out_specs=(VMEM, VMEM),
            compiler_params=params,
        )(owner, blocks, olds[0], olds[1], olds[2])
    with jax.named_scope("to_owners"):
        received = exchange(payload, "dp")
    with jax.named_scope("squares"):
        squares = jnp.sum(received[:, 64:72, :].astype(jnp.float32), axis=0)
        squares = jnp.broadcast_to(squares, (sections,) + squares.shape)
        squares = exchange(squares, "section")
    with jax.named_scope("columns"):
        copies = pl.pallas_call(
            functools.partial(column_kernel, layout, numel),
            out_shape=jax.ShapeDtypeStruct((YS, rows, narrow), jnp.bfloat16),
            in_specs=[SMEM, VMEM, VMEM, VMEM],
            out_specs=VMEM,
            scratch_shapes=[pltpu.VMEM((rows, narrow), jnp.float32)] * 4,
            compiler_params=params,
        )(owner, squares, mean, received)
    with jax.named_scope("gather_y"):
        gathered = exchange(copies, "dp", axis_index_groups=along_y)
    with jax.named_scope("gather_x"):
        copies = pl.pallas_call(
            copies_kernel,
            out_shape=jax.ShapeDtypeStruct((XS,) + gathered.shape, jnp.bfloat16),
            in_specs=[VMEM],
            out_specs=VMEM,
            compiler_params=params,
        )(gathered)
        gathered = exchange(copies, "dp", axis_index_groups=along_x)
    with jax.named_scope("finish"):
        outs = pl.pallas_call(
            functools.partial(finish_kernel, layout, numel),
            out_shape=(jax.ShapeDtypeStruct((1, rows, width), jnp.bfloat16),)
            + (jax.ShapeDtypeStruct(master.shape, jnp.float32),) * 4,
            in_specs=[SMEM] + [VMEM] * 7,
            out_specs=(HBM,) * 5,
            scratch_shapes=[pltpu.VMEM(master.shape[2:], jnp.float32)] * 4
            + [pltpu.SemaphoreType.DMA((replicas,)), pltpu.SemaphoreType.DMA((4, 4))],
            compiler_params=params,
        )(
            owner, squares, received, master, moment, second, average,
            gathered.reshape(replicas, rows, narrow),
        )
    return tuple(outs)


def solution(mesh):
    in_specs = (
        P("section", "dp", None, None),
        P("section", None),
        P("section", "dp", None, None),
        P("section", "dp", None, None),
        P("section", "dp", None, None),
        P("section", "dp", None, None),
    )
    out_specs = (
        P("section", None, None),
        P("section", "dp", None, None),
        P("section", "dp", None, None),
        P("section", "dp", None, None),
        P("section", "dp", None, None),
    )
    return jax.shard_map(local, mesh=mesh, in_specs=in_specs, out_specs=out_specs, check_vma=False)
```

```python
import functools

import jax
import jax.numpy as jnp
from jax import lax
from jax.experimental import pallas as pl
from jax.experimental.pallas import tpu as pltpu
from jax.sharding import PartitionSpec as P

STEP = 10

beta_one = 0.9
beta_two = 0.95
epsilon = 1e-08
learn_rate = 0.0003
decay_rate = 0.1
average_keep = 0.999
clip_level = 0.5

XS = 4
YS = 8


def tensor_layout(all_rows, slot_rows, layers):
    layer_rows = all_rows // layers
    kv_rows = (layer_rows - 2 - 2 * slot_rows) // 2
    counts = [slot_rows, kv_rows, kv_rows, slot_rows, 1, 1]
    layout = []
    start = 0
    for layer in range(layers):
        for position, count in enumerate(counts):
            layout.append((start, count, 1.0 if position < 4 else 0.0))
            start = start + count
    return layout


def adamw_moments(grad, moment, second, factor):
    clipped = factor * grad
    moment_new = beta_one * moment + (1.0 - beta_one) * clipped
    second_new = beta_two * second + (1.0 - beta_two) * clipped * clipped
    return moment_new, second_new


def adamw_master(master, moment_new, second_new, decay):
    direction = (moment_new * (1.0 / (1.0 - beta_one**STEP))) / (
        jnp.sqrt(second_new * (1.0 / (1.0 - beta_two**STEP))) + epsilon
    )
    return master - learn_rate * (direction + decay_rate * decay * master)


def clip_factor(squares, numel):
    return jnp.minimum(1.0, clip_level / jnp.sqrt(squares / numel + 1e-06))


def split_kernel(layout, replicas, owner, parts, master, moment, second, mean, payload):
    rows, width = mean.shape
    half = width // 2
    total = parts[0].astype(jnp.float32)
    for part in range(1, parts.shape[0]):
        total = total + parts[part].astype(jnp.float32)
    own = total / replicas
    mean[...] = own
    squared = own * own
    partial = squared[0:8]
    for row in range(8, rows, 8):
        partial = partial + squared[row : row + 8]
    partial = partial[:, :half] + partial[:, half:]
    partial = partial[0:4] + partial[4:8]
    high = partial.astype(jnp.bfloat16).astype(jnp.float32)
    squares = jnp.concatenate([high, partial - high], axis=0).astype(jnp.bfloat16)
    empty = jnp.zeros((16, half), jnp.bfloat16)
    for device in range(replicas):
        payload[device, 0:16, :] = empty
        for place, state in enumerate((moment, second, master)):
            block = jnp.concatenate(
                [
                    state[:, device * width : device * width + half],
                    state[:, device * width + half : (device + 1) * width],
                ],
                axis=0,
            )
            payload[device, 16 * place + 16 : 16 * place + 32, :] = block.astype(jnp.bfloat16)
        payload[device, 64:72, :] = squares
    for tensor, (start, count, flag) in enumerate(layout):
        block = mean[start : start + count, :]
        if count < 8:
            block = jnp.concatenate(
                [block, jnp.zeros((8 - count, width), jnp.float32)], axis=0
            )
        payload[owner[tensor], 0:16, :] = jnp.concatenate(
            [block[:, :half], block[:, half:]], axis=0
        ).astype(jnp.bfloat16)


def column_kernel(layout, numel, owner, squares, mean, received, copies, master, moment, second, decay):
    factor = clip_factor(jnp.sum(squares[...]), numel)
    half = mean.shape[1] // 2
    for tensor, (start, count, flag) in enumerate(layout):
        root = owner[tensor]
        rows = slice(start, start + count)
        for place, state in enumerate((moment, second, master)):
            block = received[root, 16 * place + 16 : 16 * place + 32, :].astype(jnp.float32)
            state[rows, :half] = block[:count]
            state[rows, half:] = block[8 : 8 + count]
        decay[rows, :] = jnp.full((count, decay.shape[1]), flag, jnp.float32)
    moment_new, second_new = adamw_moments(mean[...], moment[...], second[...], factor)
    weights = adamw_master(master[...], moment_new, second_new, decay[...])
    weights = weights.astype(jnp.bfloat16)
    for copy in range(copies.shape[0]):
        copies[copy] = weights


def owner_kernel(
    layout, numel, owner, squares, received, master, moment, second, average,
    master_out, moment_out, second_out, average_out, done,
):
    factor = clip_factor(jnp.sum(squares[...]), numel)
    me = lax.axis_index("dp")
    count = jnp.int32(0)
    flag = jnp.float32(0.0)
    for tensor, (start, rows, decay) in enumerate(layout):
        mine = owner[tensor] == me
        count = jnp.where(mine, rows, count)
        flag = jnp.where(mine, decay, flag)
    width = 2 * received.shape[2]
    used = lax.broadcasted_iota(jnp.int32, (8, width), 0) < count
    for source in range(received.shape[0]):
        columns = slice(source * width, (source + 1) * width)
        grad = received[source, 0:16, :].astype(jnp.float32)
        grad = jnp.concatenate([grad[0:8], grad[8:16]], axis=1)
        olds = (master[:, columns], moment[:, columns], second[:, columns], average[:, columns])
        moment_new, second_new = adamw_moments(grad, olds[1], olds[2], factor)
        master_new = adamw_master(olds[0], moment_new, second_new, flag)
        average_new = average_keep * olds[3] + (1.0 - average_keep) * master_new
        master_out[:, columns] = jnp.where(used, master_new, olds[0])
        moment_out[:, columns] = jnp.where(used, moment_new, olds[1])
        second_out[:, columns] = jnp.where(used, second_new, olds[2])
        average_out[:, columns] = jnp.where(used, average_new, olds[3])
    done[...] = jnp.zeros_like(done)


def cut_kernel(grads, blocks, sems):
    parts, _, width = blocks.shape
    moves = [
        pltpu.make_async_copy(
            grads.at[0, 0, :, pl.ds(part * width, width)], blocks.at[part], sems.at[part]
        )
        for part in range(parts)
    ]
    for move in moves:
        move.start()
    for move in moves:
        move.wait()


def copies_kernel(block, after, copies):
    for copy in range(copies.shape[0]):
        copies[copy] = block[...]


def join_kernel(blocks, weights, sems):
    parts, _, width = blocks.shape
    moves = [
        pltpu.make_async_copy(
            blocks.at[part], weights.at[0, :, pl.ds(part * width, width)], sems.at[part]
        )
        for part in range(parts)
    ]
    for move in moves:
        move.start()
    for move in moves:
        move.wait()


VMEM = pl.BlockSpec(memory_space=pltpu.VMEM)
HBM = pl.BlockSpec(memory_space=pltpu.HBM)
SMEM = pl.BlockSpec(memory_space=pltpu.SMEM)
LIMIT = 32 * 1024 * 1024


def local(grads, owners, master, moment, second, average):
    rows = grads.shape[2]
    width = grads.shape[3]
    layout = tensor_layout(rows, master.shape[2], owners.shape[1] // 6)
    replicas = lax.axis_size("dp")
    sections = lax.axis_size("section")
    numel = sections * rows * width
    owner = owners[0]
    along_x = [[x * YS + y for x in range(XS)] for y in range(YS)]
    along_y = [[x * YS + y for y in range(YS)] for x in range(XS)]
    exchange = functools.partial(lax.all_to_all, split_axis=0, concat_axis=0, tiled=True)
    params = pltpu.CompilerParams(vmem_limit_bytes=LIMIT)
    olds = (master[0, 0], moment[0, 0], second[0, 0], average[0, 0])
    narrow = width // replicas
    wide = width // XS

    with jax.named_scope("reduce_x"):
        blocks = pl.pallas_call(
            cut_kernel,
            out_shape=jax.ShapeDtypeStruct((XS, rows, wide), jnp.bfloat16),
            in_specs=[HBM],
            out_specs=VMEM,
            scratch_shapes=[pltpu.SemaphoreType.DMA((XS,))],
            compiler_params=pltpu.CompilerParams(vmem_limit_bytes=LIMIT),
        )(grads)
        blocks = exchange(blocks, "dp", axis_index_groups=along_x)
        summed = jnp.sum(blocks.astype(jnp.float32), axis=0).astype(jnp.bfloat16)
    with jax.named_scope("reduce_y"):
        blocks = summed.reshape(rows, YS, narrow).transpose(1, 0, 2)
        blocks = exchange(blocks, "dp", axis_index_groups=along_y)
    with jax.named_scope("split"):
        mean, payload = pl.pallas_call(
            functools.partial(split_kernel, layout, replicas),
            out_shape=(
                jax.ShapeDtypeStruct((rows, narrow), jnp.float32),
                jax.ShapeDtypeStruct((replicas, 72, narrow // 2), jnp.bfloat16),
            ),
            in_specs=[SMEM, VMEM, VMEM, VMEM, VMEM],
            out_specs=(VMEM, VMEM),
            compiler_params=params,
        )(owner, blocks, olds[0], olds[1], olds[2])
    with jax.named_scope("to_owners"):
        received = exchange(payload, "dp")
    with jax.named_scope("squares"):
        squares = jnp.sum(received[:, 64:72, :].astype(jnp.float32), axis=0)
        squares = jnp.broadcast_to(squares, (sections,) + squares.shape)
        squares = exchange(squares, "section")
    with jax.named_scope("columns"):
        copies = pl.pallas_call(
            functools.partial(column_kernel, layout, numel),
            out_shape=jax.ShapeDtypeStruct((YS, rows, narrow), jnp.bfloat16),
            in_specs=[SMEM, VMEM, VMEM, VMEM],
            out_specs=VMEM,
            scratch_shapes=[pltpu.VMEM((rows, narrow), jnp.float32)] * 4,
            compiler_params=params,
        )(owner, squares, mean, received)
    with jax.named_scope("gather_y"):
        gathered = exchange(copies, "dp", axis_index_groups=along_y)
    with jax.named_scope("owned"):
        state = jax.ShapeDtypeStruct(olds[0].shape, jnp.float32)
        *news, done = pl.pallas_call(
            functools.partial(owner_kernel, layout, numel),
            out_shape=(state,) * 4 + (jax.ShapeDtypeStruct((8, 128), jnp.float32),),
            in_specs=[SMEM] + [VMEM] * 6,
            out_specs=(VMEM,) * 5,
            compiler_params=params,
        )(owner, squares, received, *olds)
    with jax.named_scope("gather_x"):
        copies = pl.pallas_call(
            copies_kernel,
            out_shape=jax.ShapeDtypeStruct((XS,) + gathered.shape, jnp.bfloat16),
            in_specs=[VMEM, VMEM],
            out_specs=VMEM,
            compiler_params=params,
        )(gathered, done)
        gathered = exchange(copies, "dp", axis_index_groups=along_x)
    with jax.named_scope("join"):
        weights = pl.pallas_call(
            join_kernel,
            out_shape=jax.ShapeDtypeStruct((1, rows, width), jnp.bfloat16),
            in_specs=[VMEM],
            out_specs=HBM,
            scratch_shapes=[pltpu.SemaphoreType.DMA((replicas,))],
            compiler_params=params,
        )(gathered.reshape(replicas, rows, narrow))
    return (weights,) + tuple(new[None, None] for new in news)


def solution(mesh):
    in_specs = (
        P("section", "dp", None, None),
        P("section", None),
        P("section", "dp", None, None),
        P("section", "dp", None, None),
        P("section", "dp", None, None),
        P("section", "dp", None, None),
    )
    out_specs = (
        P("section", None, None),
        P("section", "dp", None, None),
        P("section", "dp", None, None),
        P("section", "dp", None, None),
        P("section", "dp", None, None),
    )
    return jax.shard_map(local, mesh=mesh, in_specs=in_specs, out_specs=out_specs, check_vma=False)
```

```python
import functools

import jax
import jax.numpy as jnp
from jax import lax
from jax.experimental import pallas as pl
from jax.experimental.pallas import tpu as pltpu
from jax.sharding import PartitionSpec as P

STEP = 10

beta_one = 0.9
beta_two = 0.95
epsilon = 1e-08
learn_rate = 0.0003
decay_rate = 0.1
average_keep = 0.999
clip_level = 0.5

XS = 4
YS = 8
CORES = 2

REDUCE_X = (1, 0, 0)
REDUCE_Y = (7, 0, 0)
SPREAD = (15, 0, 0)
SQUARES = (5, 0, 0)
GATHER_Y = (6, 0, 0)
GATHER_X = (2, 0, 0)


def tensor_layout(all_rows, slot_rows, layers):
    layer_rows = all_rows // layers
    kv_rows = (layer_rows - 2 - 2 * slot_rows) // 2
    counts = [slot_rows, kv_rows, kv_rows, slot_rows, 1, 1]
    layout = []
    start = 0
    for layer in range(layers):
        for position, count in enumerate(counts):
            layout.append((start, count, 1.0 if position < 4 else 0.0))
            start = start + count
    return layout


def first_of(turn, core, other):
    return turn[0] + turn[1] * core + turn[2] * other


def groups_along(axis, turn, sections):
    replicas = XS * YS
    groups = []
    for section in range(sections):
        base, core = section * replicas, section % CORES
        if axis == "x":
            for y in range(YS):
                first = first_of(turn, core, y)
                groups.append([base + (x + first) % XS * YS + y for x in range(XS)])
        elif axis == "y":
            for x in range(XS):
                first = first_of(turn, core, x)
                groups.append([base + x * YS + (y + first) % YS for y in range(YS)])
        else:
            first = first_of(turn, core, 0)
            groups.append([base + (index + first) % replicas for index in range(replicas)])
    return groups


def place_of(position, axis, turn):
    core = lax.rem(lax.axis_index("section"), CORES)
    me = lax.axis_index("dp")
    size, other = {
        "x": (XS, lax.rem(me, YS)), "y": (YS, lax.div(me, YS)), "dp": (XS * YS, 0),
    }[axis]
    return lax.rem(position + first_of(turn, core, other), size)


def near_place(far, near):
    core = lax.rem(lax.axis_index("section"), CORES)
    return lax.rem(near + first_of(GATHER_Y, core, place_of(far, "x", GATHER_X)), YS)


def position_of(place):
    core = lax.rem(lax.axis_index("section"), CORES)
    size = XS * YS
    return lax.rem(place + size - lax.rem(first_of(SPREAD, core, 0), size), size)


def adamw_moments(grad, moment, second, factor):
    clipped = factor * grad
    moment_new = beta_one * moment + (1.0 - beta_one) * clipped
    second_new = beta_two * second + (1.0 - beta_two) * clipped * clipped
    return moment_new, second_new


def adamw_master(master, moment_new, second_new, decay):
    direction = (moment_new * (1.0 / (1.0 - beta_one**STEP))) / (
        jnp.sqrt(second_new * (1.0 / (1.0 - beta_two**STEP))) + epsilon
    )
    return master - learn_rate * (direction + decay_rate * decay * master)


def clip_factor(squares, numel):
    return jnp.minimum(1.0, clip_level / jnp.sqrt(squares / numel + 1e-06))


def split_kernel(layout, replicas, owner, parts, master, moment, second, mean, payload):
    rows, width = mean.shape
    half = width // 2
    total = parts[0].astype(jnp.float32)
    for part in range(1, parts.shape[0]):
        total = total + parts[part].astype(jnp.float32)
    own = total / replicas
    mean[...] = own
    squared = own * own
    partial = squared[0:8]
    for row in range(8, rows, 8):
        partial = partial + squared[row : row + 8]
    partial = partial[:, :half] + partial[:, half:]
    partial = partial[0:4] + partial[4:8]
    high = partial.astype(jnp.bfloat16).astype(jnp.float32)
    squares = jnp.concatenate([high, partial - high], axis=0).astype(jnp.bfloat16)
    empty = jnp.zeros((16, half), jnp.bfloat16)
    for device in range(replicas):
        payload[device, 0:16, :] = empty
        start = pl.multiple_of(place_of(device, "dp", SPREAD) * width, width)
        for place, state in enumerate((moment, second, master)):
            block = state[:, pl.ds(start, width)]
            block = jnp.concatenate([block[:, :half], block[:, half:]], axis=0)
            payload[device, 16 * place + 16 : 16 * place + 32, :] = block.astype(jnp.bfloat16)
        payload[device, 64:72, :] = squares
    for tensor, (start, count, flag) in enumerate(layout):
        block = mean[start : start + count, :]
        if count < 8:
            block = jnp.concatenate(
                [block, jnp.zeros((8 - count, width), jnp.float32)], axis=0
            )
        payload[position_of(owner[tensor]), 0:16, :] = jnp.concatenate(
            [block[:, :half], block[:, half:]], axis=0
        ).astype(jnp.bfloat16)


def column_kernel(layout, numel, owner, squares, mean, received, copies, master, moment, second, decay):
    factor = clip_factor(jnp.sum(squares[...]), numel)
    half = mean.shape[1] // 2
    for tensor, (start, count, flag) in enumerate(layout):
        root = position_of(owner[tensor])
        rows = slice(start, start + count)
        for place, state in enumerate((moment, second, master)):
            block = received[root, 16 * place + 16 : 16 * place + 32, :].astype(jnp.float32)
            state[rows, :half] = block[:count]
            state[rows, half:] = block[8 : 8 + count]
        decay[rows, :] = jnp.full((count, decay.shape[1]), flag, jnp.float32)
    moment_new, second_new = adamw_moments(mean[...], moment[...], second[...], factor)
    weights = adamw_master(master[...], moment_new, second_new, decay[...])
    weights = weights.astype(jnp.bfloat16)
    for copy in range(copies.shape[0]):
        copies[copy] = weights


def finish_kernel(
    layout, numel, owner, squares, received, master, moment, second, average, blocks,
    weights, master_out, moment_out, second_out, average_out,
    master_new, moment_new, second_new, average_new, weight_sems, state_sems,
):
    _, _, _, width = blocks.shape
    parts = received.shape[0]
    moves = []
    for far in range(XS):
        for near in range(YS):
            start = place_of(far, "x", GATHER_X) * YS + near_place(far, near)
            moves.append(
                pltpu.make_async_copy(
                    blocks.at[far, near],
                    weights.at[0, :, pl.ds(pl.multiple_of(start * width, width), width)],
                    weight_sems.at[far, near],
                )
            )
            moves[-1].start()
    factor = clip_factor(jnp.sum(squares[...]), numel)
    me = lax.axis_index("dp")
    count = jnp.int32(0)
    flag = jnp.float32(0.0)
    for tensor, (start, height, decay) in enumerate(layout):
        mine = owner[tensor] == me
        count = jnp.where(mine, height, count)
        flag = jnp.where(mine, decay, flag)
    used = lax.broadcasted_iota(jnp.int32, (8, width), 0) < count
    pairs = (
        (master_new, master_out), (moment_new, moment_out),
        (second_new, second_out), (average_new, average_out),
    )
    pieces = 4
    stretch = parts * width // pieces
    for piece in range(pieces):
        for source in range(piece * parts // pieces, (piece + 1) * parts // pieces):
            start = pl.multiple_of(place_of(source, "dp", SPREAD) * width, width)
            columns = pl.ds(start, width)
            grad = received[source, 0:16, :].astype(jnp.float32)
            grad = jnp.concatenate([grad[0:8], grad[8:16]], axis=1)
            olds = (
                master[0, 0, :, columns], moment[0, 0, :, columns],
                second[0, 0, :, columns], average[0, 0, :, columns],
            )
            first, squared = adamw_moments(grad, olds[1], olds[2], factor)
            stepped = adamw_master(olds[0], first, squared, flag)
            mixed = average_keep * olds[3] + (1.0 - average_keep) * stepped
            for (target, _), new, old in zip(pairs, (stepped, first, squared, mixed), olds):
                target[:, columns] = jnp.where(used, new, old)
    for piece in range(pieces):
        for place, (source, target) in enumerate(pairs):
            columns = pl.ds(piece * stretch, stretch)
            moves.append(
                pltpu.make_async_copy(
                    source.at[:, columns], target.at[0, 0, :, columns], state_sems.at[place, piece]
                )
            )
            moves[-1].start()
    for move in moves:
        move.wait()


def cut_kernel(grads, blocks, sems):
    parts, _, width = blocks.shape
    moves = []
    for part in range(parts):
        start = pl.multiple_of(place_of(part, "x", REDUCE_X) * width, width)
        moves.append(
            pltpu.make_async_copy(
                grads.at[0, 0, :, pl.ds(start, width)], blocks.at[part], sems.at[part]
            )
        )
        moves[-1].start()
    for move in moves:
        move.wait()


def sum_kernel(parts, blocks):
    count, _, width = blocks.shape
    for position in range(count):
        start = pl.multiple_of(place_of(position, "y", REDUCE_Y) * width, width)
        columns = pl.ds(start, width)
        total = parts[0, :, columns].astype(jnp.float32)
        for part in range(1, parts.shape[0]):
            total = total + parts[part, :, columns].astype(jnp.float32)
        blocks[position] = total.astype(jnp.bfloat16)


def copies_kernel(block, copies):
    for copy in range(copies.shape[0]):
        copies[copy] = block[...]


VMEM = pl.BlockSpec(memory_space=pltpu.VMEM)
HBM = pl.BlockSpec(memory_space=pltpu.HBM)
SMEM = pl.BlockSpec(memory_space=pltpu.SMEM)
LIMIT = 32 * 1024 * 1024


def local(grads, owners, master, moment, second, average):
    rows = grads.shape[2]
    width = grads.shape[3]
    layout = tensor_layout(rows, master.shape[2], owners.shape[1] // 6)
    replicas = lax.axis_size("dp")
    sections = lax.axis_size("section")
    numel = sections * rows * width
    owner = owners[0]
    everyone = ("section", "dp")
    planes = sections // CORES
    all_sections = [
        [
            (plane + SQUARES[0]) % planes * CORES + core
            for plane in range(planes)
            for core in range(CORES)
        ]
    ]
    exchange = functools.partial(lax.all_to_all, split_axis=0, concat_axis=0, tiled=True)
    params = pltpu.CompilerParams(vmem_limit_bytes=LIMIT)
    olds = (master[0, 0], moment[0, 0], second[0, 0], average[0, 0])
    narrow = width // replicas
    wide = width // XS

    with jax.named_scope("reduce_x"):
        blocks = pl.pallas_call(
            cut_kernel,
            out_shape=pltpu.VMEM((XS, rows, wide), jnp.bfloat16),
            in_specs=[HBM],
            out_specs=VMEM,
            scratch_shapes=[pltpu.SemaphoreType.DMA((XS,))],
            compiler_params=pltpu.CompilerParams(vmem_limit_bytes=LIMIT),
        )(pltpu.with_memory_space_constraint(grads, pltpu.HBM))
        blocks = exchange(blocks, everyone, axis_index_groups=groups_along("x", REDUCE_X, sections))
    with jax.named_scope("reduce_y"):
        blocks = pl.pallas_call(
            sum_kernel,
            out_shape=jax.ShapeDtypeStruct((YS, rows, narrow), jnp.bfloat16),
            in_specs=[VMEM],
            out_specs=VMEM,
            compiler_params=params,
        )(blocks)
        blocks = exchange(blocks, everyone, axis_index_groups=groups_along("y", REDUCE_Y, sections))
    with jax.named_scope("split"):
        mean, payload = pl.pallas_call(
            functools.partial(split_kernel, layout, replicas),
            out_shape=(
                jax.ShapeDtypeStruct((rows, narrow), jnp.float32),
                jax.ShapeDtypeStruct((replicas, 72, narrow // 2), jnp.bfloat16),
            ),
            in_specs=[SMEM, VMEM, VMEM, VMEM, VMEM],
            out_specs=(VMEM, VMEM),
            compiler_params=params,
        )(owner, blocks, olds[0], olds[1], olds[2])
    with jax.named_scope("to_owners"):
        received = exchange(payload, everyone, axis_index_groups=groups_along("dp", SPREAD, sections))
    with jax.named_scope("squares"):
        squares = jnp.sum(received[:, 64:72, :].astype(jnp.float32), axis=0)
        squares = jnp.broadcast_to(squares, (sections,) + squares.shape)
        squares = exchange(squares, "section", axis_index_groups=all_sections)
    with jax.named_scope("columns"):
        copies = pl.pallas_call(
            functools.partial(column_kernel, layout, numel),
            out_shape=jax.ShapeDtypeStruct((YS, rows, narrow), jnp.bfloat16),
            in_specs=[SMEM, VMEM, VMEM, VMEM],
            out_specs=VMEM,
            scratch_shapes=[pltpu.VMEM((rows, narrow), jnp.float32)] * 4,
            compiler_params=params,
        )(owner, squares, mean, received)
    with jax.named_scope("gather_y"):
        gathered = exchange(copies, everyone, axis_index_groups=groups_along("y", GATHER_Y, sections))
    with jax.named_scope("gather_x"):
        copies = pl.pallas_call(
            copies_kernel,
            out_shape=jax.ShapeDtypeStruct((XS,) + gathered.shape, jnp.bfloat16),
            in_specs=[VMEM],
            out_specs=VMEM,
            compiler_params=params,
        )(gathered)
        gathered = exchange(copies, everyone, axis_index_groups=groups_along("x", GATHER_X, sections))
    with jax.named_scope("finish"):
        outs = pl.pallas_call(
            functools.partial(finish_kernel, layout, numel),
            out_shape=(jax.ShapeDtypeStruct((1, rows, width), jnp.bfloat16),)
            + (jax.ShapeDtypeStruct(master.shape, jnp.float32),) * 4,
            in_specs=[SMEM] + [VMEM] * 7,
            out_specs=(HBM,) * 5,
            scratch_shapes=[pltpu.VMEM(master.shape[2:], jnp.float32)] * 4
            + [pltpu.SemaphoreType.DMA((XS, YS)), pltpu.SemaphoreType.DMA((4, 4))],
            compiler_params=params,
        )(
            owner, squares, received, master, moment, second, average,
            gathered,
        )
    return tuple(outs)


def solution(mesh):
    in_specs = (
        P("section", "dp", None, None),
        P("section", None),
        P("section", "dp", None, None),
        P("section", "dp", None, None),
        P("section", "dp", None, None),
        P("section", "dp", None, None),
    )
    out_specs = (
        P("section", None, None),
        P("section", "dp", None, None),
        P("section", "dp", None, None),
        P("section", "dp", None, None),
        P("section", "dp", None, None),
    )
    return jax.shard_map(local, mesh=mesh, in_specs=in_specs, out_specs=out_specs, check_vma=False)
```

```python
import functools

import jax
import jax.numpy as jnp
from jax import lax
from jax.experimental import pallas as pl
from jax.experimental.pallas import tpu as pltpu
from jax.sharding import PartitionSpec as P

STEP = 10

beta_one = 0.9
beta_two = 0.95
epsilon = 1e-08
learn_rate = 0.0003
decay_rate = 0.1
average_keep = 0.999
clip_level = 0.5

XS = 4
YS = 8
CORES = 2

REDUCE_X = (1, 0, 0, -1)
REDUCE_Y = (6, 0, 0, 1)
SPREAD = (14, 0, 0, 1)
SQUARES = (5, 0, 0, -1)
GATHER_Y = (5, 0, 0, 1)
GATHER_X = (2, 0, 0, -1)


def tensor_layout(all_rows, slot_rows, layers):
    layer_rows = all_rows // layers
    kv_rows = (layer_rows - 2 - 2 * slot_rows) // 2
    counts = [slot_rows, kv_rows, kv_rows, slot_rows, 1, 1]
    layout = []
    start = 0
    for layer in range(layers):
        for position, count in enumerate(counts):
            layout.append((start, count, 1.0 if position < 4 else 0.0))
            start = start + count
    return layout


def first_of(turn, core, other):
    return turn[0] + turn[1] * core + turn[2] * other


def groups_along(axis, turn, sections):
    replicas = XS * YS
    groups = []
    for section in range(sections):
        base, core = section * replicas, section % CORES
        if axis == "x":
            for y in range(YS):
                first = first_of(turn, core, y)
                groups.append([base + (turn[3] * x + first) % XS * YS + y for x in range(XS)])
        elif axis == "y":
            for x in range(XS):
                first = first_of(turn, core, x)
                groups.append([base + x * YS + (turn[3] * y + first) % YS for y in range(YS)])
        else:
            first = first_of(turn, core, 0)
            groups.append([base + (turn[3] * index + first) % replicas for index in range(replicas)])
    return groups


def place_of(position, axis, turn):
    core = lax.rem(lax.axis_index("section"), CORES)
    me = lax.axis_index("dp")
    size, other = {
        "x": (XS, lax.rem(me, YS)), "y": (YS, lax.div(me, YS)), "dp": (XS * YS, 0),
    }[axis]
    return lax.rem(size + turn[3] * position + first_of(turn, core, other), size)


def near_place(far, near):
    core = lax.rem(lax.axis_index("section"), CORES)
    return lax.rem(YS + GATHER_Y[3] * near + first_of(GATHER_Y, core, place_of(far, "x", GATHER_X)), YS)


def position_of(place):
    core = lax.rem(lax.axis_index("section"), CORES)
    size = XS * YS
    return lax.rem(size + SPREAD[3] * (place - lax.rem(first_of(SPREAD, core, 0), size)), size)


def adamw_moments(grad, moment, second, factor):
    clipped = factor * grad
    moment_new = beta_one * moment + (1.0 - beta_one) * clipped
    second_new = beta_two * second + (1.0 - beta_two) * clipped * clipped
    return moment_new, second_new


def adamw_master(master, moment_new, second_new, decay):
    direction = (moment_new * (1.0 / (1.0 - beta_one**STEP))) / (
        jnp.sqrt(second_new * (1.0 / (1.0 - beta_two**STEP))) + epsilon
    )
    return master - learn_rate * (direction + decay_rate * decay * master)


def clip_factor(squares, numel):
    return jnp.minimum(1.0, clip_level / jnp.sqrt(squares / numel + 1e-06))


def split_kernel(layout, replicas, owner, parts, master, moment, second, mean, payload):
    rows, width = mean.shape
    half = width // 2
    total = parts[0].astype(jnp.float32)
    for part in range(1, parts.shape[0]):
        total = total + parts[part].astype(jnp.float32)
    own = total / replicas
    mean[...] = own
    squared = own * own
    partial = squared[0:8]
    for row in range(8, rows, 8):
        partial = partial + squared[row : row + 8]
    partial = partial[:, :half] + partial[:, half:]
    partial = partial[0:4] + partial[4:8]
    high = partial.astype(jnp.bfloat16).astype(jnp.float32)
    squares = jnp.concatenate([high, partial - high], axis=0).astype(jnp.bfloat16)
    empty = jnp.zeros((16, half), jnp.bfloat16)
    for device in range(replicas):
        payload[device, 0:16, :] = empty
        start = pl.multiple_of(place_of(device, "dp", SPREAD) * width, width)
        for place, state in enumerate((moment, second, master)):
            block = state[:, pl.ds(start, width)]
            block = jnp.concatenate([block[:, :half], block[:, half:]], axis=0)
            payload[device, 16 * place + 16 : 16 * place + 32, :] = block.astype(jnp.bfloat16)
        payload[device, 64:72, :] = squares
    for tensor, (start, count, flag) in enumerate(layout):
        block = mean[start : start + count, :]
        if count < 8:
            block = jnp.concatenate(
                [block, jnp.zeros((8 - count, width), jnp.float32)], axis=0
            )
        payload[position_of(owner[tensor]), 0:16, :] = jnp.concatenate(
            [block[:, :half], block[:, half:]], axis=0
        ).astype(jnp.bfloat16)


def column_kernel(layout, numel, owner, squares, mean, received, copies, master, moment, second, decay):
    factor = clip_factor(jnp.sum(squares[...]), numel)
    half = mean.shape[1] // 2
    for tensor, (start, count, flag) in enumerate(layout):
        root = position_of(owner[tensor])
        rows = slice(start, start + count)
        for place, state in enumerate((moment, second, master)):
            block = received[root, 16 * place + 16 : 16 * place + 32, :].astype(jnp.float32)
            state[rows, :half] = block[:count]
            state[rows, half:] = block[8 : 8 + count]
        decay[rows, :] = jnp.full((count, decay.shape[1]), flag, jnp.float32)
    moment_new, second_new = adamw_moments(mean[...], moment[...], second[...], factor)
    weights = adamw_master(master[...], moment_new, second_new, decay[...])
    weights = weights.astype(jnp.bfloat16)
    for copy in range(copies.shape[0]):
        copies[copy] = weights


def finish_kernel(
    layout, numel, owner, squares, received, master, moment, second, average, blocks,
    weights, master_out, moment_out, second_out, average_out,
    master_new, moment_new, second_new, average_new, weight_sems, state_sems,
):
    _, _, _, width = blocks.shape
    parts = received.shape[0]
    moves = []
    for far in range(XS):
        for near in range(YS):
            start = place_of(far, "x", GATHER_X) * YS + near_place(far, near)
            moves.append(
                pltpu.make_async_copy(
                    blocks.at[far, near],
                    weights.at[0, :, pl.ds(pl.multiple_of(start * width, width), width)],
                    weight_sems.at[far, near],
                )
            )
            moves[-1].start()
    factor = clip_factor(jnp.sum(squares[...]), numel)
    me = lax.axis_index("dp")
    count = jnp.int32(0)
    flag = jnp.float32(0.0)
    for tensor, (start, height, decay) in enumerate(layout):
        mine = owner[tensor] == me
        count = jnp.where(mine, height, count)
        flag = jnp.where(mine, decay, flag)
    used = lax.broadcasted_iota(jnp.int32, (8, width), 0) < count
    pairs = (
        (master_new, master_out), (moment_new, moment_out),
        (second_new, second_out), (average_new, average_out),
    )
    pieces = 4
    stretch = parts * width // pieces
    for piece in range(pieces):
        for source in range(piece * parts // pieces, (piece + 1) * parts // pieces):
            start = pl.multiple_of(place_of(source, "dp", SPREAD) * width, width)
            columns = pl.ds(start, width)
            grad = received[source, 0:16, :].astype(jnp.float32)
            grad = jnp.concatenate([grad[0:8], grad[8:16]], axis=1)
            olds = (
                master[0, 0, :, columns], moment[0, 0, :, columns],
                second[0, 0, :, columns], average[0, 0, :, columns],
            )
            first, squared = adamw_moments(grad, olds[1], olds[2], factor)
            stepped = adamw_master(olds[0], first, squared, flag)
            mixed = average_keep * olds[3] + (1.0 - average_keep) * stepped
            for (target, _), new, old in zip(pairs, (stepped, first, squared, mixed), olds):
                target[:, columns] = jnp.where(used, new, old)
    for piece in range(pieces):
        for place, (source, target) in enumerate(pairs):
            columns = pl.ds(piece * stretch, stretch)
            moves.append(
                pltpu.make_async_copy(
                    source.at[:, columns], target.at[0, 0, :, columns], state_sems.at[place, piece]
                )
            )
            moves[-1].start()
    for move in moves:
        move.wait()


def cut_kernel(grads, blocks, sems):
    parts, _, width = blocks.shape
    moves = []
    for part in range(parts):
        start = pl.multiple_of(place_of(part, "x", REDUCE_X) * width, width)
        moves.append(
            pltpu.make_async_copy(
                grads.at[0, 0, :, pl.ds(start, width)], blocks.at[part], sems.at[part]
            )
        )
        moves[-1].start()
    for move in moves:
        move.wait()


def sum_kernel(parts, blocks):
    count, _, width = blocks.shape
    for position in range(count):
        start = pl.multiple_of(place_of(position, "y", REDUCE_Y) * width, width)
        columns = pl.ds(start, width)
        total = parts[0, :, columns].astype(jnp.float32)
        for part in range(1, parts.shape[0]):
            total = total + parts[part, :, columns].astype(jnp.float32)
        blocks[position] = total.astype(jnp.bfloat16)


def copies_kernel(block, copies):
    for copy in range(copies.shape[0]):
        copies[copy] = block[...]


VMEM = pl.BlockSpec(memory_space=pltpu.VMEM)
HBM = pl.BlockSpec(memory_space=pltpu.HBM)
SMEM = pl.BlockSpec(memory_space=pltpu.SMEM)
LIMIT = 32 * 1024 * 1024


def local(grads, owners, master, moment, second, average):
    rows = grads.shape[2]
    width = grads.shape[3]
    layout = tensor_layout(rows, master.shape[2], owners.shape[1] // 6)
    replicas = lax.axis_size("dp")
    sections = lax.axis_size("section")
    numel = sections * rows * width
    owner = owners[0]
    everyone = ("section", "dp")
    planes = sections // CORES
    all_sections = [
        [
            (SQUARES[3] * plane + SQUARES[0]) % planes * CORES + core
            for plane in range(planes)
            for core in range(CORES)
        ]
    ]
    exchange = functools.partial(lax.all_to_all, split_axis=0, concat_axis=0, tiled=True)
    params = pltpu.CompilerParams(vmem_limit_bytes=LIMIT)
    olds = (master[0, 0], moment[0, 0], second[0, 0], average[0, 0])
    narrow = width // replicas
    wide = width // XS

    with jax.named_scope("reduce_x"):
        blocks = pl.pallas_call(
            cut_kernel,
            out_shape=pltpu.VMEM((XS, rows, wide), jnp.bfloat16),
            in_specs=[HBM],
            out_specs=VMEM,
            scratch_shapes=[pltpu.SemaphoreType.DMA((XS,))],
            compiler_params=pltpu.CompilerParams(vmem_limit_bytes=LIMIT),
        )(pltpu.with_memory_space_constraint(grads, pltpu.HBM))
        blocks = exchange(blocks, everyone, axis_index_groups=groups_along("x", REDUCE_X, sections))
    with jax.named_scope("reduce_y"):
        blocks = pl.pallas_call(
            sum_kernel,
            out_shape=jax.ShapeDtypeStruct((YS, rows, narrow), jnp.bfloat16),
            in_specs=[VMEM],
            out_specs=VMEM,
            compiler_params=params,
        )(blocks)
        blocks = exchange(blocks, everyone, axis_index_groups=groups_along("y", REDUCE_Y, sections))
    with jax.named_scope("split"):
        mean, payload = pl.pallas_call(
            functools.partial(split_kernel, layout, replicas),
            out_shape=(
                jax.ShapeDtypeStruct((rows, narrow), jnp.float32),
                jax.ShapeDtypeStruct((replicas, 72, narrow // 2), jnp.bfloat16),
            ),
            in_specs=[SMEM, VMEM, VMEM, VMEM, VMEM],
            out_specs=(VMEM, VMEM),
            compiler_params=params,
        )(owner, blocks, olds[0], olds[1], olds[2])
    with jax.named_scope("to_owners"):
        received = exchange(payload, everyone, axis_index_groups=groups_along("dp", SPREAD, sections))
    with jax.named_scope("squares"):
        squares = jnp.sum(received[:, 64:72, :].astype(jnp.float32), axis=0)
        squares = jnp.broadcast_to(squares, (sections,) + squares.shape)
        squares = exchange(squares, "section", axis_index_groups=all_sections)
    with jax.named_scope("columns"):
        copies = pl.pallas_call(
            functools.partial(column_kernel, layout, numel),
            out_shape=jax.ShapeDtypeStruct((YS, rows, narrow), jnp.bfloat16),
            in_specs=[SMEM, VMEM, VMEM, VMEM],
            out_specs=VMEM,
            scratch_shapes=[pltpu.VMEM((rows, narrow), jnp.float32)] * 4,
            compiler_params=params,
        )(owner, squares, mean, received)
    with jax.named_scope("gather_y"):
        gathered = exchange(copies, everyone, axis_index_groups=groups_along("y", GATHER_Y, sections))
    with jax.named_scope("gather_x"):
        copies = pl.pallas_call(
            copies_kernel,
            out_shape=jax.ShapeDtypeStruct((XS,) + gathered.shape, jnp.bfloat16),
            in_specs=[VMEM],
            out_specs=VMEM,
            compiler_params=params,
        )(gathered)
        gathered = exchange(copies, everyone, axis_index_groups=groups_along("x", GATHER_X, sections))
    with jax.named_scope("finish"):
        outs = pl.pallas_call(
            functools.partial(finish_kernel, layout, numel),
            out_shape=(jax.ShapeDtypeStruct((1, rows, width), jnp.bfloat16),)
            + (jax.ShapeDtypeStruct(master.shape, jnp.float32),) * 4,
            in_specs=[SMEM] + [VMEM] * 7,
            out_specs=(HBM,) * 5,
            scratch_shapes=[pltpu.VMEM(master.shape[2:], jnp.float32)] * 4
            + [pltpu.SemaphoreType.DMA((XS, YS)), pltpu.SemaphoreType.DMA((4, 4))],
            compiler_params=params,
        )(
            owner, squares, received, master, moment, second, average,
            gathered,
        )
    return tuple(outs)


def solution(mesh):
    in_specs = (
        P("section", "dp", None, None),
        P("section", None),
        P("section", "dp", None, None),
        P("section", "dp", None, None),
        P("section", "dp", None, None),
        P("section", "dp", None, None),
    )
    out_specs = (
        P("section", None, None),
        P("section", "dp", None, None),
        P("section", "dp", None, None),
        P("section", "dp", None, None),
        P("section", "dp", None, None),
    )
    return jax.shard_map(local, mesh=mesh, in_specs=in_specs, out_specs=out_specs, check_vma=False)
```

```python
import functools

import jax
import jax.numpy as jnp
from jax import lax
from jax.experimental import pallas as pl
from jax.experimental.pallas import tpu as pltpu
from jax.sharding import PartitionSpec as P

STEP = 10

beta_one = 0.9
beta_two = 0.95
epsilon = 1e-08
learn_rate = 0.0003
decay_rate = 0.1
average_keep = 0.999
clip_level = 0.5

XS = 4
YS = 8
CORES = 2

REDUCE_X = (1, 0, 0, -1)
REDUCE_Y = (6, 0, 0, 1)
SPREAD = (15, 0, 0, 1)
SQUARES = (5, 0, 0, -1)
GATHER_Y = (5, 0, 0, 1)
GATHER_X = (2, 0, 0, -1)


def tensor_layout(all_rows, slot_rows, layers):
    layer_rows = all_rows // layers
    kv_rows = (layer_rows - 2 - 2 * slot_rows) // 2
    counts = [slot_rows, kv_rows, kv_rows, slot_rows, 1, 1]
    layout = []
    start = 0
    for layer in range(layers):
        for position, count in enumerate(counts):
            layout.append((start, count, 1.0 if position < 4 else 0.0))
            start = start + count
    return layout


def first_of(turn, core, other):
    return turn[0] + turn[1] * core + turn[2] * other


def groups_along(axis, turn, sections):
    replicas = XS * YS
    groups = []
    for section in range(sections):
        base, core = section * replicas, section % CORES
        if axis == "x":
            for y in range(YS):
                first = first_of(turn, core, y)
                groups.append([base + (turn[3] * x + first) % XS * YS + y for x in range(XS)])
        elif axis == "y":
            for x in range(XS):
                first = first_of(turn, core, x)
                groups.append([base + x * YS + (turn[3] * y + first) % YS for y in range(YS)])
        else:
            first = first_of(turn, core, 0)
            groups.append([base + (turn[3] * index + first) % replicas for index in range(replicas)])
    return groups


def place_of(position, axis, turn):
    core = lax.rem(lax.axis_index("section"), CORES)
    me = lax.axis_index("dp")
    size, other = {
        "x": (XS, lax.rem(me, YS)), "y": (YS, lax.div(me, YS)), "dp": (XS * YS, 0),
    }[axis]
    return lax.rem(size + turn[3] * position + first_of(turn, core, other), size)


def near_place(far, near):
    core = lax.rem(lax.axis_index("section"), CORES)
    return lax.rem(YS + GATHER_Y[3] * near + first_of(GATHER_Y, core, place_of(far, "x", GATHER_X)), YS)


def position_of(place):
    core = lax.rem(lax.axis_index("section"), CORES)
    size = XS * YS
    return lax.rem(size + SPREAD[3] * (place - lax.rem(first_of(SPREAD, core, 0), size)), size)


def adamw_moments(grad, moment, second, factor):
    clipped = factor * grad
    moment_new = beta_one * moment + (1.0 - beta_one) * clipped
    second_new = beta_two * second + (1.0 - beta_two) * clipped * clipped
    return moment_new, second_new


def adamw_master(master, moment_new, second_new, decay):
    direction = (moment_new * (1.0 / (1.0 - beta_one**STEP))) / (
        jnp.sqrt(second_new * (1.0 / (1.0 - beta_two**STEP))) + epsilon
    )
    return master - learn_rate * (direction + decay_rate * decay * master)


def clip_factor(squares, numel):
    return jnp.minimum(1.0, clip_level / jnp.sqrt(squares / numel + 1e-06))


def split_kernel(layout, replicas, owner, parts, master, moment, second, mean, payload):
    rows, width = mean.shape
    half = width // 2
    total = parts[0].astype(jnp.float32)
    for part in range(1, parts.shape[0]):
        total = total + parts[part].astype(jnp.float32)
    own = total / replicas
    mean[...] = own
    squared = own * own
    partial = squared[0:8]
    for row in range(8, rows, 8):
        partial = partial + squared[row : row + 8]
    partial = partial[:, :half] + partial[:, half:]
    partial = partial[0:4] + partial[4:8]
    high = partial.astype(jnp.bfloat16).astype(jnp.float32)
    squares = jnp.concatenate([high, partial - high], axis=0).astype(jnp.bfloat16)
    empty = jnp.zeros((16, half), jnp.bfloat16)
    for device in range(replicas):
        payload[device, 0:16, :] = empty
        start = pl.multiple_of(place_of(device, "dp", SPREAD) * width, width)
        for place, state in enumerate((moment, second, master)):
            block = state[:, pl.ds(start, width)]
            block = jnp.concatenate([block[:, :half], block[:, half:]], axis=0)
            payload[device, 16 * place + 16 : 16 * place + 32, :] = block.astype(jnp.bfloat16)
        payload[device, 64:72, :] = squares
    for tensor, (start, count, flag) in enumerate(layout):
        block = mean[start : start + count, :]
        if count < 8:
            block = jnp.concatenate(
                [block, jnp.zeros((8 - count, width), jnp.float32)], axis=0
            )
        payload[position_of(owner[tensor]), 0:16, :] = jnp.concatenate(
            [block[:, :half], block[:, half:]], axis=0
        ).astype(jnp.bfloat16)


def column_kernel(layout, numel, owner, squares, mean, received, copies, master, moment, second, decay):
    factor = clip_factor(jnp.sum(squares[...]), numel)
    half = mean.shape[1] // 2
    for tensor, (start, count, flag) in enumerate(layout):
        root = position_of(owner[tensor])
        rows = slice(start, start + count)
        for place, state in enumerate((moment, second, master)):
            block = received[root, 16 * place + 16 : 16 * place + 32, :].astype(jnp.float32)
            state[rows, :half] = block[:count]
            state[rows, half:] = block[8 : 8 + count]
        decay[rows, :] = jnp.full((count, decay.shape[1]), flag, jnp.float32)
    moment_new, second_new = adamw_moments(mean[...], moment[...], second[...], factor)
    weights = adamw_master(master[...], moment_new, second_new, decay[...])
    weights = weights.astype(jnp.bfloat16)
    for copy in range(copies.shape[0]):
        copies[copy] = weights


def finish_kernel(
    layout, numel, owner, squares, received, master, moment, second, average, blocks,
    weights, master_out, moment_out, second_out, average_out,
    master_new, moment_new, second_new, average_new, weight_sems, state_sems,
):
    _, _, _, width = blocks.shape
    parts = received.shape[0]
    moves = []
    for far in range(XS):
        for near in range(YS):
            start = place_of(far, "x", GATHER_X) * YS + near_place(far, near)
            moves.append(
                pltpu.make_async_copy(
                    blocks.at[far, near],
                    weights.at[0, :, pl.ds(pl.multiple_of(start * width, width), width)],
                    weight_sems.at[far, near],
                )
            )
            moves[-1].start()
    factor = clip_factor(jnp.sum(squares[...]), numel)
    me = lax.axis_index("dp")
    count = jnp.int32(0)
    flag = jnp.float32(0.0)
    for tensor, (start, height, decay) in enumerate(layout):
        mine = owner[tensor] == me
        count = jnp.where(mine, height, count)
        flag = jnp.where(mine, decay, flag)
    used = lax.broadcasted_iota(jnp.int32, (8, width), 0) < count
    pairs = (
        (master_new, master_out), (moment_new, moment_out),
        (second_new, second_out), (average_new, average_out),
    )
    pieces = 4
    stretch = parts * width // pieces
    for piece in range(pieces):
        for source in range(piece * parts // pieces, (piece + 1) * parts // pieces):
            start = pl.multiple_of(place_of(source, "dp", SPREAD) * width, width)
            columns = pl.ds(start, width)
            grad = received[source, 0:16, :].astype(jnp.float32)
            grad = jnp.concatenate([grad[0:8], grad[8:16]], axis=1)
            olds = (
                master[0, 0, :, columns], moment[0, 0, :, columns],
                second[0, 0, :, columns], average[0, 0, :, columns],
            )
            first, squared = adamw_moments(grad, olds[1], olds[2], factor)
            stepped = adamw_master(olds[0], first, squared, flag)
            mixed = average_keep * olds[3] + (1.0 - average_keep) * stepped
            for (target, _), new, old in zip(pairs, (stepped, first, squared, mixed), olds):
                target[:, columns] = jnp.where(used, new, old)
    for piece in range(pieces):
        for place, (source, target) in enumerate(pairs):
            columns = pl.ds(piece * stretch, stretch)
            moves.append(
                pltpu.make_async_copy(
                    source.at[:, columns], target.at[0, 0, :, columns], state_sems.at[place, piece]
                )
            )
            moves[-1].start()
    for move in moves:
        move.wait()


def cut_kernel(grads, blocks, sems):
    parts, _, width = blocks.shape
    moves = []
    for part in range(parts):
        start = pl.multiple_of(place_of(part, "x", REDUCE_X) * width, width)
        moves.append(
            pltpu.make_async_copy(
                grads.at[0, 0, :, pl.ds(start, width)], blocks.at[part], sems.at[part]
            )
        )
        moves[-1].start()
    for move in moves:
        move.wait()


def sum_kernel(parts, blocks):
    count, _, width = blocks.shape
    for position in range(count):
        start = pl.multiple_of(place_of(position, "y", REDUCE_Y) * width, width)
        columns = pl.ds(start, width)
        total = parts[0, :, columns].astype(jnp.float32)
        for part in range(1, parts.shape[0]):
            total = total + parts[part, :, columns].astype(jnp.float32)
        blocks[position] = total.astype(jnp.bfloat16)


def copies_kernel(block, copies):
    for copy in range(copies.shape[0]):
        copies[copy] = block[...]


VMEM = pl.BlockSpec(memory_space=pltpu.VMEM)
HBM = pl.BlockSpec(memory_space=pltpu.HBM)
SMEM = pl.BlockSpec(memory_space=pltpu.SMEM)
LIMIT = 32 * 1024 * 1024


def local(grads, owners, master, moment, second, average):
    rows = grads.shape[2]
    width = grads.shape[3]
    layout = tensor_layout(rows, master.shape[2], owners.shape[1] // 6)
    replicas = lax.axis_size("dp")
    sections = lax.axis_size("section")
    numel = sections * rows * width
    owner = owners[0]
    everyone = ("section", "dp")
    planes = sections // CORES
    all_sections = [
        [
            (SQUARES[3] * plane + SQUARES[0]) % planes * CORES + core
            for plane in range(planes)
            for core in range(CORES)
        ]
    ]
    exchange = functools.partial(lax.all_to_all, split_axis=0, concat_axis=0, tiled=True)
    params = pltpu.CompilerParams(vmem_limit_bytes=LIMIT)
    olds = (master[0, 0], moment[0, 0], second[0, 0], average[0, 0])
    narrow = width // replicas
    wide = width // XS

    with jax.named_scope("reduce_x"):
        blocks = pl.pallas_call(
            cut_kernel,
            out_shape=pltpu.VMEM((XS, rows, wide), jnp.bfloat16),
            in_specs=[HBM],
            out_specs=VMEM,
            scratch_shapes=[pltpu.SemaphoreType.DMA((XS,))],
            compiler_params=pltpu.CompilerParams(vmem_limit_bytes=LIMIT),
        )(pltpu.with_memory_space_constraint(grads, pltpu.HBM))
        blocks = exchange(blocks, everyone, axis_index_groups=groups_along("x", REDUCE_X, sections))
    with jax.named_scope("reduce_y"):
        blocks = pl.pallas_call(
            sum_kernel,
            out_shape=jax.ShapeDtypeStruct((YS, rows, narrow), jnp.bfloat16),
            in_specs=[VMEM],
            out_specs=VMEM,
            compiler_params=params,
        )(blocks)
        blocks = exchange(blocks, everyone, axis_index_groups=groups_along("y", REDUCE_Y, sections))
    with jax.named_scope("split"):
        mean, payload = pl.pallas_call(
            functools.partial(split_kernel, layout, replicas),
            out_shape=(
                jax.ShapeDtypeStruct((rows, narrow), jnp.float32),
                jax.ShapeDtypeStruct((replicas, 72, narrow // 2), jnp.bfloat16),
            ),
            in_specs=[SMEM, VMEM, VMEM, VMEM, VMEM],
            out_specs=(VMEM, VMEM),
            compiler_params=params,
        )(owner, blocks, olds[0], olds[1], olds[2])
    with jax.named_scope("to_owners"):
        received = exchange(payload, everyone, axis_index_groups=groups_along("dp", SPREAD, sections))
    with jax.named_scope("squares"):
        squares = jnp.sum(received[:, 64:72, :].astype(jnp.float32), axis=(0, 1))
        squares = jnp.broadcast_to(squares, (sections, 1) + squares.shape)
        squares = exchange(squares, "section", axis_index_groups=all_sections)
    with jax.named_scope("columns"):
        copies = pl.pallas_call(
            functools.partial(column_kernel, layout, numel),
            out_shape=jax.ShapeDtypeStruct((YS, rows, narrow), jnp.bfloat16),
            in_specs=[SMEM, VMEM, VMEM, VMEM],
            out_specs=VMEM,
            scratch_shapes=[pltpu.VMEM((rows, narrow), jnp.float32)] * 4,
            compiler_params=params,
        )(owner, squares, mean, received)
    with jax.named_scope("gather_y"):
        gathered = exchange(copies, everyone, axis_index_groups=groups_along("y", GATHER_Y, sections))
    with jax.named_scope("gather_x"):
        copies = pl.pallas_call(
            copies_kernel,
            out_shape=jax.ShapeDtypeStruct((XS,) + gathered.shape, jnp.bfloat16),
            in_specs=[VMEM],
            out_specs=VMEM,
            compiler_params=params,
        )(gathered)
        gathered = exchange(copies, everyone, axis_index_groups=groups_along("x", GATHER_X, sections))
    with jax.named_scope("finish"):
        outs = pl.pallas_call(
            functools.partial(finish_kernel, layout, numel),
            out_shape=(jax.ShapeDtypeStruct((1, rows, width), jnp.bfloat16),)
            + (jax.ShapeDtypeStruct(master.shape, jnp.float32),) * 4,
            in_specs=[SMEM] + [VMEM] * 7,
            out_specs=(HBM,) * 5,
            scratch_shapes=[pltpu.VMEM(master.shape[2:], jnp.float32)] * 4
            + [pltpu.SemaphoreType.DMA((XS, YS)), pltpu.SemaphoreType.DMA((4, 4))],
            compiler_params=params,
        )(
            owner, squares, received, master, moment, second, average,
            gathered,
        )
    return tuple(outs)


def solution(mesh):
    in_specs = (
        P("section", "dp", None, None),
        P("section", None),
        P("section", "dp", None, None),
        P("section", "dp", None, None),
        P("section", "dp", None, None),
        P("section", "dp", None, None),
    )
    out_specs = (
        P("section", None, None),
        P("section", "dp", None, None),
        P("section", "dp", None, None),
        P("section", "dp", None, None),
        P("section", "dp", None, None),
    )
    return jax.shard_map(local, mesh=mesh, in_specs=in_specs, out_specs=out_specs, check_vma=False)
```

```python
import functools

import jax
import jax.numpy as jnp
from jax import lax
from jax.experimental import pallas as pl
from jax.experimental.pallas import tpu as pltpu
from jax.sharding import PartitionSpec as P

STEP = 10

beta_one = 0.9
beta_two = 0.95
epsilon = 1e-08
learn_rate = 0.0003
decay_rate = 0.1
average_keep = 0.999
clip_level = 0.5

XS = 4
YS = 8
CORES = 2

REDUCE_X = (1, 0, 0, -1)
REDUCE_Y = (6, 0, 0, 1)
SPREAD = (15, 0, 0, 1)
SQUARES = (5, 0, 0, -1)
GATHER_Y = (5, 0, 0, 1)
GATHER_X = (2, 0, 0, -1)


def tensor_layout(all_rows, slot_rows, layers):
    layer_rows = all_rows // layers
    kv_rows = (layer_rows - 2 - 2 * slot_rows) // 2
    counts = [slot_rows, kv_rows, kv_rows, slot_rows, 1, 1]
    layout = []
    start = 0
    for layer in range(layers):
        for position, count in enumerate(counts):
            layout.append((start, count, 1.0 if position < 4 else 0.0))
            start = start + count
    return layout


def first_of(turn, core, other):
    return turn[0] + turn[1] * core + turn[2] * other


def groups_along(axis, turn, sections):
    replicas = XS * YS
    groups = []
    for section in range(sections):
        base, core = section * replicas, section % CORES
        if axis == "x":
            for y in range(YS):
                first = first_of(turn, core, y)
                groups.append([base + (turn[3] * x + first) % XS * YS + y for x in range(XS)])
        elif axis == "y":
            for x in range(XS):
                first = first_of(turn, core, x)
                groups.append([base + x * YS + (turn[3] * y + first) % YS for y in range(YS)])
        else:
            first = first_of(turn, core, 0)
            groups.append([base + (turn[3] * index + first) % replicas for index in range(replicas)])
    return groups


def place_of(position, axis, turn):
    core = lax.rem(lax.axis_index("section"), CORES)
    me = lax.axis_index("dp")
    size, other = {
        "x": (XS, lax.rem(me, YS)), "y": (YS, lax.div(me, YS)), "dp": (XS * YS, 0),
    }[axis]
    return lax.rem(size + turn[3] * position + first_of(turn, core, other), size)


def near_place(far, near):
    core = lax.rem(lax.axis_index("section"), CORES)
    return lax.rem(YS + GATHER_Y[3] * near + first_of(GATHER_Y, core, place_of(far, "x", GATHER_X)), YS)


def position_of(place):
    core = lax.rem(lax.axis_index("section"), CORES)
    size = XS * YS
    return lax.rem(size + SPREAD[3] * (place - lax.rem(first_of(SPREAD, core, 0), size)), size)


def adamw_moments(grad, moment, second, factor):
    clipped = factor * grad
    moment_new = beta_one * moment + (1.0 - beta_one) * clipped
    second_new = beta_two * second + (1.0 - beta_two) * clipped * clipped
    return moment_new, second_new


def adamw_master(master, moment_new, second_new, decay):
    direction = (moment_new * (1.0 / (1.0 - beta_one**STEP))) / (
        jnp.sqrt(second_new * (1.0 / (1.0 - beta_two**STEP))) + epsilon
    )
    return master - learn_rate * (direction + decay_rate * decay * master)


def clip_factor(squares, numel):
    return jnp.minimum(1.0, clip_level / jnp.sqrt(squares / numel + 1e-06))


def split_kernel(layout, replicas, owner, parts, master, moment, second, mean, payload):
    rows, width = mean.shape
    half = width // 2
    total = parts[0].astype(jnp.float32)
    for part in range(1, parts.shape[0]):
        total = total + parts[part].astype(jnp.float32)
    own = total / replicas
    mean[...] = own
    squared = own * own
    partial = squared[0:8]
    for row in range(8, rows, 8):
        partial = partial + squared[row : row + 8]
    partial = partial[:, :half] + partial[:, half:]
    partial = partial[0:4] + partial[4:8]
    high = partial.astype(jnp.bfloat16).astype(jnp.float32)
    squares = jnp.concatenate([high, partial - high], axis=0).astype(jnp.bfloat16)
    empty = jnp.zeros((16, half), jnp.bfloat16)
    for device in range(replicas):
        payload[device, 0:16, :] = empty
        start = pl.multiple_of(place_of(device, "dp", SPREAD) * width, width)
        for place, state in enumerate((moment, second, master)):
            block = state[:, pl.ds(start, width)]
            block = jnp.concatenate([block[:, :half], block[:, half:]], axis=0)
            payload[device, 16 * place + 16 : 16 * place + 32, :] = block.astype(jnp.bfloat16)
        payload[device, 64:72, :] = squares
    for tensor, (start, count, flag) in enumerate(layout):
        block = mean[start : start + count, :]
        if count < 8:
            block = jnp.concatenate(
                [block, jnp.zeros((8 - count, width), jnp.float32)], axis=0
            )
        payload[position_of(owner[tensor]), 0:16, :] = jnp.concatenate(
            [block[:, :half], block[:, half:]], axis=0
        ).astype(jnp.bfloat16)


def column_kernel(layout, numel, owner, squares, mean, received, copies, master, moment, second, decay):
    factor = clip_factor(jnp.sum(squares[...]), numel)
    half = mean.shape[1] // 2
    for tensor, (start, count, flag) in enumerate(layout):
        root = position_of(owner[tensor])
        rows = slice(start, start + count)
        for place, state in enumerate((moment, second, master)):
            block = received[root, 16 * place + 16 : 16 * place + 32, :].astype(jnp.float32)
            state[rows, :half] = block[:count]
            state[rows, half:] = block[8 : 8 + count]
        decay[rows, :] = jnp.full((count, decay.shape[1]), flag, jnp.float32)
    moment_new, second_new = adamw_moments(mean[...], moment[...], second[...], factor)
    weights = adamw_master(master[...], moment_new, second_new, decay[...])
    weights = weights.astype(jnp.bfloat16)
    for copy in range(copies.shape[0]):
        copies[copy] = weights


def finish_kernel(
    layout, numel, owner, squares, received, master, moment, second, average, blocks,
    weights, master_out, moment_out, second_out, average_out,
    whole, master_new, moment_new, second_new, average_new, weight_sems, state_sems,
):
    _, _, _, width = blocks.shape
    parts = received.shape[0]
    moves = []
    starts = [
        (far, near, place_of(far, "x", GATHER_X) * YS + near_place(far, near))
        for far in range(XS)
        for near in range(YS)
    ]
    for row in range(0, whole.shape[0], 16):
        stripe = slice(row, row + 16)
        for far, near, start in starts:
            columns = pl.ds(pl.multiple_of(start * width, width), width)
            whole[stripe, columns] = blocks[far, near, stripe, :]
        moves.append(
            pltpu.make_async_copy(
                whole.at[pl.ds(row, 16)], weights.at[0, pl.ds(row, 16)], weight_sems.at[row // 16]
            )
        )
        moves[-1].start()
    factor = clip_factor(jnp.sum(squares[...]), numel)
    me = lax.axis_index("dp")
    count = jnp.int32(0)
    flag = jnp.float32(0.0)
    for tensor, (start, height, decay) in enumerate(layout):
        mine = owner[tensor] == me
        count = jnp.where(mine, height, count)
        flag = jnp.where(mine, decay, flag)
    used = lax.broadcasted_iota(jnp.int32, (8, width), 0) < count
    pairs = (
        (master_new, master_out), (moment_new, moment_out),
        (second_new, second_out), (average_new, average_out),
    )
    pieces = 4
    stretch = parts * width // pieces
    for piece in range(pieces):
        for source in range(piece * parts // pieces, (piece + 1) * parts // pieces):
            start = pl.multiple_of(place_of(source, "dp", SPREAD) * width, width)
            columns = pl.ds(start, width)
            grad = received[source, 0:16, :].astype(jnp.float32)
            grad = jnp.concatenate([grad[0:8], grad[8:16]], axis=1)
            olds = (
                master[0, 0, :, columns], moment[0, 0, :, columns],
                second[0, 0, :, columns], average[0, 0, :, columns],
            )
            first, squared = adamw_moments(grad, olds[1], olds[2], factor)
            stepped = adamw_master(olds[0], first, squared, flag)
            mixed = average_keep * olds[3] + (1.0 - average_keep) * stepped
            for (target, _), new, old in zip(pairs, (stepped, first, squared, mixed), olds):
                target[:, columns] = jnp.where(used, new, old)
    for piece in range(pieces):
        for place, (source, target) in enumerate(pairs):
            columns = pl.ds(piece * stretch, stretch)
            moves.append(
                pltpu.make_async_copy(
                    source.at[:, columns], target.at[0, 0, :, columns], state_sems.at[place, piece]
                )
            )
            moves[-1].start()
    for move in moves:
        move.wait()


def cut_kernel(grads, blocks, sems):
    parts, _, width = blocks.shape
    moves = []
    for part in range(parts):
        start = pl.multiple_of(place_of(part, "x", REDUCE_X) * width, width)
        moves.append(
            pltpu.make_async_copy(
                grads.at[0, 0, :, pl.ds(start, width)], blocks.at[part], sems.at[part]
            )
        )
        moves[-1].start()
    for move in moves:
        move.wait()


def sum_kernel(parts, blocks):
    count, _, width = blocks.shape
    for position in range(count):
        start = pl.multiple_of(place_of(position, "y", REDUCE_Y) * width, width)
        columns = pl.ds(start, width)
        total = parts[0, :, columns].astype(jnp.float32)
        for part in range(1, parts.shape[0]):
            total = total + parts[part, :, columns].astype(jnp.float32)
        blocks[position] = total.astype(jnp.bfloat16)


def copies_kernel(block, copies):
    for copy in range(copies.shape[0]):
        copies[copy] = block[...]


VMEM = pl.BlockSpec(memory_space=pltpu.VMEM)
HBM = pl.BlockSpec(memory_space=pltpu.HBM)
SMEM = pl.BlockSpec(memory_space=pltpu.SMEM)
LIMIT = 32 * 1024 * 1024


def local(grads, owners, master, moment, second, average):
    rows = grads.shape[2]
    width = grads.shape[3]
    layout = tensor_layout(rows, master.shape[2], owners.shape[1] // 6)
    replicas = lax.axis_size("dp")
    sections = lax.axis_size("section")
    numel = sections * rows * width
    owner = owners[0]
    everyone = ("section", "dp")
    planes = sections // CORES
    all_sections = [
        [
            (SQUARES[3] * plane + SQUARES[0]) % planes * CORES + core
            for core in range(CORES)
            for plane in range(planes)
        ]
    ]
    exchange = functools.partial(lax.all_to_all, split_axis=0, concat_axis=0, tiled=True)
    params = pltpu.CompilerParams(vmem_limit_bytes=LIMIT)
    olds = (master[0, 0], moment[0, 0], second[0, 0], average[0, 0])
    narrow = width // replicas
    wide = width // XS

    with jax.named_scope("reduce_x"):
        blocks = pl.pallas_call(
            cut_kernel,
            out_shape=pltpu.VMEM((XS, rows, wide), jnp.bfloat16),
            in_specs=[HBM],
            out_specs=VMEM,
            scratch_shapes=[pltpu.SemaphoreType.DMA((XS,))],
            compiler_params=pltpu.CompilerParams(vmem_limit_bytes=LIMIT),
        )(pltpu.with_memory_space_constraint(grads, pltpu.HBM))
        blocks = exchange(blocks, everyone, axis_index_groups=groups_along("x", REDUCE_X, sections))
    with jax.named_scope("reduce_y"):
        blocks = pl.pallas_call(
            sum_kernel,
            out_shape=jax.ShapeDtypeStruct((YS, rows, narrow), jnp.bfloat16),
            in_specs=[VMEM],
            out_specs=VMEM,
            compiler_params=params,
        )(blocks)
        blocks = exchange(blocks, everyone, axis_index_groups=groups_along("y", REDUCE_Y, sections))
    with jax.named_scope("split"):
        mean, payload = pl.pallas_call(
            functools.partial(split_kernel, layout, replicas),
            out_shape=(
                jax.ShapeDtypeStruct((rows, narrow), jnp.float32),
                jax.ShapeDtypeStruct((replicas, 72, narrow // 2), jnp.bfloat16),
            ),
            in_specs=[SMEM, VMEM, VMEM, VMEM, VMEM],
            out_specs=(VMEM, VMEM),
            compiler_params=params,
        )(owner, blocks, olds[0], olds[1], olds[2])
    with jax.named_scope("to_owners"):
        received = exchange(payload, everyone, axis_index_groups=groups_along("dp", SPREAD, sections))
    with jax.named_scope("squares"):
        squares = jnp.sum(received[:, 64:72, :].astype(jnp.float32), axis=(0, 1))
        squares = jnp.broadcast_to(squares, (sections, 1) + squares.shape)
        squares = exchange(squares, "section", axis_index_groups=all_sections)
    with jax.named_scope("columns"):
        copies = pl.pallas_call(
            functools.partial(column_kernel, layout, numel),
            out_shape=jax.ShapeDtypeStruct((YS, rows, narrow), jnp.bfloat16),
            in_specs=[SMEM, VMEM, VMEM, VMEM],
            out_specs=VMEM,
            scratch_shapes=[pltpu.VMEM((rows, narrow), jnp.float32)] * 4,
            compiler_params=params,
        )(owner, squares, mean, received)
    with jax.named_scope("gather_y"):
        gathered = exchange(copies, everyone, axis_index_groups=groups_along("y", GATHER_Y, sections))
    with jax.named_scope("gather_x"):
        copies = pl.pallas_call(
            copies_kernel,
            out_shape=jax.ShapeDtypeStruct((XS,) + gathered.shape, jnp.bfloat16),
            in_specs=[VMEM],
            out_specs=VMEM,
            compiler_params=params,
        )(gathered)
        gathered = exchange(copies, everyone, axis_index_groups=groups_along("x", GATHER_X, sections))
    with jax.named_scope("finish"):
        outs = pl.pallas_call(
            functools.partial(finish_kernel, layout, numel),
            out_shape=(jax.ShapeDtypeStruct((1, rows, width), jnp.bfloat16),)
            + (jax.ShapeDtypeStruct(master.shape, jnp.float32),) * 4,
            in_specs=[SMEM] + [VMEM] * 7,
            out_specs=(HBM,) * 5,
            scratch_shapes=[pltpu.VMEM((rows, width), jnp.bfloat16)]
            + [pltpu.VMEM(master.shape[2:], jnp.float32)] * 4
            + [pltpu.SemaphoreType.DMA((rows // 16,)), pltpu.SemaphoreType.DMA((4, 4))],
            compiler_params=params,
        )(
            owner, squares, received, master, moment, second, average,
            gathered,
        )
    return tuple(outs)


def solution(mesh):
    in_specs = (
        P("section", "dp", None, None),
        P("section", None),
        P("section", "dp", None, None),
        P("section", "dp", None, None),
        P("section", "dp", None, None),
        P("section", "dp", None, None),
    )
    out_specs = (
        P("section", None, None),
        P("section", "dp", None, None),
        P("section", "dp", None, None),
        P("section", "dp", None, None),
        P("section", "dp", None, None),
    )
    return jax.shard_map(local, mesh=mesh, in_specs=in_specs, out_specs=out_specs, check_vma=False)
```
